32 devices in a mesh: ctx: 8 (over y, x, core), wt: 4 (over z).
Axes of the slice: x: 2, y: 2, z: 4, core: 2. Of those that a mesh axis runs over, the one named last changes fastest.
Arguments:
- hidden_in: bfloat16 [4, 1280, 896], P('wt', 'ctx'), may hold values from -6 to 6
- positions: int32 [4, 1280], P('wt', 'ctx'), may hold values from 0 to 1279, as said below
- cotangent: bfloat16 [4, 1280, 896], P('wt', 'ctx'), may hold values from -6 to 6
- attn_gain: bfloat16 [2, 896], P(None, ('ctx', 'wt')), may hold values from 0.5 to 1.5
- qkv_weight: bfloat16 [2, 896, 1152], P(None, ('ctx', 'wt')), may hold values from -0.25 to 0.25
- qkv_bias: bfloat16 [2, 1152], P(None, ('ctx', 'wt')), may hold values from -3 to 3
- out_weight: bfloat16 [2, 896, 896], P(None, ('ctx', 'wt')), may hold values from -1 to 1
- mlp_gain: bfloat16 [2, 896], P(None, ('ctx', 'wt')), may hold values from 0.5 to 1.5
- in_weight: bfloat16 [2, 896, 9728], P(None, ('ctx', 'wt')), may hold values from -0.1875 to 0.1875
- down_weight: bfloat16 [2, 4864, 896], P(None, ('ctx', 'wt')), may hold values from -0.15625 to 0.15625
Outputs:
- hidden_out: float32 [4, 1280, 896], P('wt', 'ctx')
- input_grad: float32 [4, 1280, 896], P('wt', 'ctx')
- attn_gain_grad: float32 [2, 896], P(None, ('ctx', 'wt'))
- qkv_weight_grad: float32 [2, 896, 1152], P(None, ('ctx', 'wt'))
- qkv_bias_grad: float32 [2, 1152], P(None, ('ctx', 'wt'))
- out_weight_grad: float32 [2, 896, 896], P(None, ('ctx', 'wt'))
- mlp_gain_grad: float32 [2, 896], P(None, ('ctx', 'wt'))
- in_weight_grad: float32 [2, 896, 9728], P(None, ('ctx', 'wt'))
- down_weight_grad: float32 [2, 4864, 896], P(None, ('ctx', 'wt'))
The draws below stay inside these ranges and needn't reach their ends.
Inputs may be any that keep to these rules, and one draw needn't show every extreme that they name: Each row of positions holds every value of 0 to 1279 once, as 16 runs of 80 consecutive ascending values, each run starting at a multiple of 80 and at a column that is a multiple of 80; the order of the runs differs from row to row.
All inputs are finite; a program needn't handle non-finite values.
Results may differ from the reference program's by a relative error of at most 0.025.
Values may be sent and summed in bfloat16 or wider, within the bound.
No kernel may reach another device: no remote copies, remote signals or barrier semaphores. Data moves between devices by JAX's collectives and lax.ppermute only.
A program may use at most 448 MiB of HBM per device.

```python
import math
import jax
import jax.numpy as jnp
from jax import lax

D = 896
HEADS = 14
KV_HEADS = 2
HEAD = 64
FF = 4864
LAYERS = 2
QW = 896
QKV_W = 1152
SEQS = 4
LEN = 1280
SPAN = 80
SPANS = 16


def draw_positions(key, part):
    key = jax.random.fold_in(key, 7)
    seq_keys = jax.random.split(key, SEQS)

    def one_row(row_key):
        order = jax.random.permutation(row_key, SPANS).astype(jnp.int32)
        within = jnp.arange(SPAN, dtype=jnp.int32)
        return (order[:, None] * SPAN + within[None, :]).reshape(-1)
    return jax.vmap(one_row)(seq_keys).astype(jnp.int32)


def raised(drawn, own_key, source, target, parts, factor):
    owner, partner = [(jnp.arange(drawn.shape[position]) // (drawn.shape[position] // parts)).reshape([-1 if axis == position else 1 for axis in range(drawn.ndim)]) for position in (source, target)]
    chosen = jax.random.permutation(own_key, parts)[partner]
    strong = (owner == chosen) | (owner == (partner + parts // 2) % parts)
    return jnp.where(strong, factor * drawn, drawn)


def level_of(own_key, extent, shards, least, high):
    level = 1.0
    for dim, blocks in shards:
        draws = jax.random.uniform(jax.random.fold_in(jax.random.fold_in(own_key, 6), dim), (blocks,), jnp.float32, least / len(shards), high / len(shards))
        level = level * jnp.repeat(jnp.exp(draws), extent[dim] // blocks).reshape((-1,) + (1,) * (len(extent) - 1 - dim))
    return level


def noise(own_key, dims, spread, bound, cuts=(), held_as=jnp.bfloat16):
    values = spread * jax.random.normal(own_key, dims, jnp.float32)
    if cuts:
        values = values * level_of(own_key, dims, cuts, -0.22, 0.18)
    return jnp.clip(values, -bound, bound).astype(held_as)


def gaussian_with(rng, extent, spread, reach, cuts, heavy, kind=jnp.bfloat16):
    array = spread * jax.random.normal(rng, extent, jnp.float32)
    if cuts:
        array = array * level_of(rng, extent, cuts, -0.22, 0.18)
    return jnp.clip(raised(array, jax.random.fold_in(rng, 3), *heavy), -reach, reach).astype(kind)


def setup_inputs(seed: int = 0) -> dict:
    seeds = jax.random.split(jax.random.key(seed), 11)
    return {
        "hidden_in": noise(seeds[0], (SEQS, LEN, D), 1.0, 6.0, ((0, 4), (1, 8))),
        "positions": draw_positions(jax.random.fold_in(seeds[10], 71), 0),
        "cotangent": gaussian_with(seeds[2], (SEQS, LEN, D), 1.0, 6.0, ((0, 4), (1, 8)), (1, 2, 8, 2.0)),
        "attn_gain": jnp.clip(1.0 + 0.1 * jax.random.normal(seeds[3], (LAYERS, D), jnp.float32), 0.5, 1.5).astype(jnp.bfloat16),
        "qkv_weight": noise(seeds[4], (LAYERS, D, QKV_W), (D // 2) ** -0.5, 0.25, ((1, 32),)),
        "qkv_bias": noise(seeds[5], (LAYERS, QKV_W), 0.5, 3.0, ((1, 32),)),
        "out_weight": noise(seeds[6], (LAYERS, QW, D), (HEAD // 2) ** -0.5, 1.0, ((1, 32),)),
        "mlp_gain": jnp.clip(1.0 + 0.1 * jax.random.normal(seeds[7], (LAYERS, D), jnp.float32), 0.5, 1.5).astype(jnp.bfloat16),
        "in_weight": noise(seeds[8], (LAYERS, D, 2 * FF), D ** -0.5, 0.1875, ((1, 32),)),
        "down_weight": noise(seeds[9], (LAYERS, FF, D), (FF // 4) ** -0.5, 0.15625, ((1, 32),)),
    }


EPSILON = 1e-06
ROPE_BASE = 1000000.0
NEGATIVE = -1e+30
PRECISE = lax.Precision.HIGHEST

@jax.custom_vjp
def low(v):
    return lax.optimization_barrier(v.astype(jnp.bfloat16)).astype(jnp.float32)

@jax.custom_vjp
def low_back(v):
    return v

def low_keep(v):
    return (low(v), None)

def low_pass(kept, grad):
    return (grad,)

def back_keep(v):
    return (v, None)

def back_low(kept, grad):
    return (low(grad),)
low.defvjp(low_keep, low_pass)
low_back.defvjp(back_keep, back_low)

def norm_rows(hidden, norm_gain):
    return hidden * lax.rsqrt(lax.optimization_barrier(jnp.mean(hidden * hidden, axis=-1, keepdims=True)) + EPSILON) * norm_gain

def rope_tables(own_positions):
    half_head = HEAD // 2
    frequency = jnp.exp(jnp.arange(half_head, dtype=jnp.float32) * (-2.0 * math.log(ROPE_BASE) / HEAD))
    angles = own_positions.astype(jnp.float32)[:, None] * frequency[None, :]
    cos_half = jnp.cos(angles)
    sin_half = jnp.sin(angles)
    return (jnp.concatenate([cos_half, cos_half], axis=-1), jnp.concatenate([sin_half, sin_half], axis=-1))

def rotate(tensor, cos_table, sin_table):
    half_head = HEAD // 2
    turned = jnp.concatenate([-tensor[..., half_head:], tensor[..., :half_head]], axis=-1)
    return tensor * cos_table[:, None, :] + turned * sin_table[:, None, :]

def attend(pieces):
    queries, all_keys, all_values, seq_positions = pieces
    row_count = queries.shape[0]
    grouped = queries.reshape(row_count, KV_HEADS, HEADS // KV_HEADS, HEAD)
    scores = jnp.einsum('tkgd,skd->tkgs', grouped, all_keys, precision=PRECISE) * HEAD ** (-0.5)
    scores = low_back(scores)
    allowed = seq_positions[None, :] <= seq_positions[:, None]
    scores = jnp.where(allowed[:, None, None, :], scores, NEGATIVE)
    row_max = lax.optimization_barrier(jnp.max(scores, axis=-1, keepdims=True))
    exponent = jnp.exp(scores - row_max)
    attn_probs = exponent / lax.optimization_barrier(jnp.sum(exponent, axis=-1, keepdims=True))
    head_mix = jnp.einsum('tkgs,skd->tkgd', low(attn_probs), all_values, precision=PRECISE)
    return head_mix.reshape(row_count, HEADS * HEAD)

def forward(hidden_in, attn_gain, qkv_weight, qkv_bias, out_weight, mlp_gain, in_weight, down_weight, positions):
    seq_count = hidden_in.shape[0]
    seq_len = hidden_in.shape[1]
    hidden = hidden_in.reshape(seq_count * seq_len, D)
    cos_table, sin_table = rope_tables(positions.reshape(-1))
    kv_cols = KV_HEADS * HEAD
    for layer_idx in range(LAYERS):
        normed = low(norm_rows(hidden, attn_gain[layer_idx]))
        packed = low_back(jnp.dot(normed, qkv_weight[layer_idx], precision=PRECISE) + qkv_bias[layer_idx])
        queries = low(rotate(packed[:, :QW].reshape(-1, HEADS, HEAD), cos_table, sin_table))
        key_rows = low(rotate(packed[:, QW:QW + kv_cols].reshape(-1, KV_HEADS, HEAD), cos_table, sin_table))
        value_rows = low(packed[:, QW + kv_cols:].reshape(-1, KV_HEADS, HEAD))
        head_mix = lax.map(jax.checkpoint(attend), (queries.reshape(seq_count, seq_len, HEADS, HEAD), key_rows.reshape(seq_count, seq_len, KV_HEADS, HEAD), value_rows.reshape(seq_count, seq_len, KV_HEADS, HEAD), positions))
        heads_out = low(low_back(head_mix.reshape(seq_count * seq_len, QW)))
        hidden = hidden + low_back(jnp.dot(heads_out, out_weight[layer_idx], precision=PRECISE))
        normed2 = low(norm_rows(hidden, mlp_gain[layer_idx]))
        gate_up = low_back(jnp.dot(normed2, in_weight[layer_idx], precision=PRECISE))
        activated = low(jax.nn.silu(gate_up[:, :FF]) * gate_up[:, FF:])
        hidden = hidden + low_back(jnp.dot(activated, down_weight[layer_idx], precision=PRECISE))
    return hidden.reshape(seq_count, seq_len, D)

def reference(hidden_in, positions, cotangent, attn_gain, qkv_weight, qkv_bias, out_weight, mlp_gain, in_weight, down_weight):
    primals = (hidden_in.astype(jnp.float32), attn_gain.astype(jnp.float32), qkv_weight.astype(jnp.float32), qkv_bias.astype(jnp.float32), out_weight.astype(jnp.float32), mlp_gain.astype(jnp.float32), in_weight.astype(jnp.float32), down_weight.astype(jnp.float32))

    def run(*values):
        return forward(*values, positions)
    hidden_out, pullback = jax.vjp(run, *primals)
    grads = pullback(cotangent.astype(jnp.float32))
    return (hidden_out, grads[0], grads[1], grads[2], grads[3], grads[4], grads[5], grads[6], grads[7])
```

```python
import math

import jax
import jax.numpy as jnp
from jax import lax
from jax.sharding import PartitionSpec as P

HEADS = 14
KV_HEADS = 2
HEAD = 64
FF = 4864
LAYERS = 2
QW = 896
D = 896
QKV_W = 1152
KV_W = KV_HEADS * HEAD

EPSILON = 1e-06
ROPE_BASE = 1000000.0
NEGATIVE = -1e30

bf16 = jnp.bfloat16
f32 = jnp.float32


def norm_rows(hidden, norm_gain):
    return (
        hidden * lax.rsqrt(jnp.mean(hidden * hidden, axis=-1, keepdims=True) + EPSILON) * norm_gain
    )


def rope_tables(own_positions):
    half_head = HEAD // 2
    frequency = jnp.exp(
        jnp.arange(half_head, dtype=jnp.float32) * (-2.0 * math.log(ROPE_BASE) / HEAD)
    )
    angles = own_positions.astype(jnp.float32)[:, None] * frequency[None, :]
    cos_half = jnp.cos(angles)
    sin_half = jnp.sin(angles)
    return (
        jnp.concatenate([cos_half, cos_half], axis=-1),
        jnp.concatenate([sin_half, sin_half], axis=-1),
    )


def rotate(tensor, cos_table, sin_table):
    half_head = HEAD // 2
    turned = jnp.concatenate([-tensor[..., half_head:], tensor[..., :half_head]], axis=-1)
    return tensor * cos_table[:, None, :] + turned * sin_table[:, None, :]


def dot(left, right):
    return jnp.dot(left, right, preferred_element_type=f32)


def dot_rows(left, right):
    return lax.dot_general(left, right, (((0,), (0,)), ((), ())), preferred_element_type=f32)


def dot_cols(left, right):
    return lax.dot_general(left, right, (((1,), (1,)), ((), ())), preferred_element_type=f32)


class Ring:
    def __init__(self, n, m):
        self.n, self.m = n, m
        if n == 8:
            self.even = [0, 4, 2, 6, 1, 3, 5, 7]
            self.odd = [0, 2, 4, 6, 1, 5, 3, 7]
        else:
            self.even = self.odd = list(range(n))

    def swap(self, value, offset, odd_offset=None):
        odd_offset = offset if odd_offset is None else odd_offset
        return lax.ppermute(
            value, "ctx", [(i, i ^ (odd_offset if i % 2 else offset)) for i in range(self.n)]
        )

    def swap_z(self, value, offset):
        return lax.ppermute(value, "wt", [(i, i ^ offset) for i in range(self.m)])

    def offsets(self, me):
        table = jnp.where(
            me % 2 == 1, jnp.array(self.odd, jnp.int32), jnp.array(self.even, jnp.int32)
        )
        return table

    def gather(self, own):
        if self.n == 8:
            blocks = [own, self.swap(own, 4, 2), self.swap(own, 2, 4), self.swap(own, 6)]
            return jnp.stack(blocks + [self.swap(b, 1) for b in blocks])
        blocks = own[None]
        step = 1
        while step < self.n:
            blocks = jnp.concatenate([blocks, self.swap(blocks, step)])
            step *= 2
        return blocks

    def reduce(self, terms):
        if self.n == 8:
            half = terms[:4].astype(f32) + self.swap(terms[4:], 1).astype(f32)
            quarter = half[:2] + self.swap(half[2:].astype(bf16), 2, 4).astype(f32)
            return quarter[0] + self.swap(quarter[1].astype(bf16), 4, 2).astype(f32)
        step = self.n // 2
        total = terms.astype(f32)
        while step:
            total = total[:step] + self.swap(total[step:].astype(bf16), step).astype(f32)
            step //= 2
        return total[0]

    def gather_z(self, own):
        return jnp.stack([own] + [self.swap_z(own, k) for k in range(1, self.m)])

    def reduce_z(self, terms):
        total = terms[0].astype(f32)
        for k in range(1, self.m):
            total = total + self.swap_z(terms[k].astype(bf16), k).astype(f32)
        return total


def make_body(n, m):
    ring = Ring(n, m)
    rows = D // (n * m)
    bias_w = QKV_W // (n * m)
    pad_rows = -(-(rows + 2) // 8) * 8
    all_rows = n * m * pad_rows
    units = FF // n
    unit_pad = -(-units // 128) * 128

    def gather_rows(block):
        return ring.gather(ring.gather_z(block)).reshape(all_rows, block.shape[-1])

    def reduce_rows(terms):
        width = terms.shape[-1]
        part = ring.reduce(terms.astype(bf16).reshape(n, m * pad_rows, width))
        return ring.reduce_z(part.reshape(m, pad_rows, width))

    def feed_in(in_weight_layer):
        cut = in_weight_layer.reshape(rows, 2, n, units).transpose(2, 0, 1, 3)
        cut = jnp.pad(cut, ((0, 0), (0, 0), (0, 0), (0, unit_pad - units)))
        cut = cut.reshape(n, rows, 2 * unit_pad)
        got = lax.all_to_all(cut, "ctx", 0, 0, tiled=True).reshape(n * rows, 2 * unit_pad)
        full = lax.all_gather(got, "wt", axis=0, tiled=True)
        full = full.reshape(m, n, rows, 2 * unit_pad).transpose(1, 0, 2, 3)
        return full.reshape(D, 2 * unit_pad)

    def feed_in_terms(grad):
        terms = grad.astype(bf16).reshape(n, m, rows, 2 * unit_pad).transpose(1, 0, 2, 3)
        terms = terms.reshape(D, 2 * unit_pad)
        return lax.psum_scatter(terms, "wt", scatter_dimension=0, tiled=True)

    def feed_in_home(parts):
        cut = jnp.stack([p.reshape(n, rows, 2 * unit_pad) for p in parts], axis=1)
        got = lax.all_to_all(cut, "ctx", 0, 0, tiled=True)
        got = got.reshape(n, LAYERS, rows, 2, unit_pad)[..., :units].astype(f32)
        return got.transpose(1, 2, 3, 0, 4).reshape(LAYERS, rows, 2 * FF)

    def body(
        hidden_in,
        positions,
        cotangent,
        attn_gain,
        qkv_weight,
        qkv_bias,
        out_weight,
        mlp_gain,
        in_weight,
        down_weight,
    ):
        me, me_z = lax.axis_index("ctx"), lax.axis_index("wt")
        shard = me * m + me_z
        offsets = ring.offsets(me)
        own_positions = positions[0]
        row_count = own_positions.shape[0]

        bias_rows = [
            lax.dynamic_update_slice(
                jnp.zeros((1, QKV_W), bf16), qkv_bias[l][None], (0, shard * bias_w)
            )
            for l in range(LAYERS)
        ]

        def qkv_block(l):
            gains = jnp.zeros((1, QKV_W), bf16)
            gains = lax.dynamic_update_slice(gains, attn_gain[l][None], (0, 0))
            gains = lax.dynamic_update_slice(gains, mlp_gain[l][None], (0, 128))
            rest = jnp.zeros((pad_rows - rows - 2, QKV_W), bf16)
            return jnp.concatenate([qkv_weight[l], bias_rows[l], gains, rest])

        def out_block(l):
            return jnp.pad(out_weight[l], ((0, pad_rows - rows), (0, 0)))

        joint = [gather_rows(qkv_block(l)) for l in range(LAYERS)]
        out_proj = [gather_rows(out_block(l)) for l in range(LAYERS)]

        column = jnp.arange(all_rows, dtype=jnp.int32)
        in_block, block = column % pad_rows, column // pad_rows
        block_owner = ((me ^ offsets[:, None]) * m + (me_z ^ jnp.arange(m))[None, :]).reshape(-1)
        owner = jnp.repeat(block_owner, pad_rows)
        feature = jnp.where(in_block < rows, owner * rows + in_block, -1)
        perm = (jnp.arange(D, dtype=jnp.int32)[:, None] == feature[None, :]).astype(bf16)
        ones_column = (in_block == rows).astype(bf16)[None, :]

        def to_rel(value):
            return dot(value, perm).astype(bf16)

        def from_rel(value):
            return dot_cols(value, perm)

        def gains_of(l):
            kept = joint[l].reshape(n * m, pad_rows, QKV_W)[:, rows + 1, :]
            both = jnp.stack([kept[:, :pad_rows], kept[:, 128 : 128 + pad_rows]])
            return from_rel(both.reshape(2, all_rows))

        gains = [gains_of(l) for l in range(LAYERS)]
        in_proj = [feed_in(in_weight[l]) for l in range(LAYERS)]
        down_proj = [
            lax.all_gather(down_weight[l], "wt", axis=0, tiled=True) for l in range(LAYERS)
        ]

        positions_by_index = lax.all_gather(own_positions, "ctx", axis=0, tiled=False)
        all_positions = positions_by_index[me ^ offsets].reshape(-1)
        cos_table, sin_table = rope_tables(own_positions)
        allowed = all_positions[None, :] <= own_positions[:, None]

        cotangent_low = ring.gather(cotangent[0]).reshape(n * row_count, D)

        def grouped_scores(queries, all_keys):
            grouped = queries.reshape(row_count, KV_HEADS, HEADS // KV_HEADS, HEAD)
            scores = jnp.einsum(
                "tkgd,skd->tkgs", grouped, all_keys, preferred_element_type=f32
            ) * HEAD ** (-0.5)
            return (grouped, jnp.where(allowed[:, None, None, :], scores, NEGATIVE))

        def attention_forward(hidden, l):
            normed = norm_rows(hidden, gains[l][0]).astype(bf16)
            normed_rel = to_rel(normed) + ones_column
            packed = dot(normed_rel, joint[l])
            queries = rotate(
                packed[:, :QW].reshape(row_count, HEADS, HEAD), cos_table, sin_table
            ).astype(bf16)
            own_keys = rotate(
                packed[:, QW : QW + KV_W].reshape(row_count, KV_HEADS, HEAD), cos_table, sin_table
            ).astype(bf16)
            own_kv = jnp.concatenate(
                [own_keys.reshape(row_count, KV_W), packed[:, QW + KV_W :].astype(bf16)], axis=1
            )
            all_kv = ring.gather(own_kv).reshape(n * row_count, 2, KV_HEADS, HEAD)
            all_keys, all_values = all_kv[:, 0], all_kv[:, 1]
            grouped, scores = grouped_scores(queries, all_keys)
            row_max = jnp.max(scores, axis=-1, keepdims=True)
            exponent = jnp.exp(scores - row_max)
            row_sum = jnp.sum(exponent, axis=-1, keepdims=True)
            attn_probs = (exponent / row_sum).astype(bf16)
            head_mix = jnp.einsum(
                "tkgs,skd->tkgd", attn_probs, all_values, preferred_element_type=f32
            )
            heads_rel = to_rel(head_mix.reshape(row_count, QW).astype(bf16))
            middle = hidden + dot(heads_rel, out_proj[l])
            return middle, (normed_rel, queries, all_keys, all_values, row_max, row_sum, heads_rel)

        def mlp_forward(middle, l):
            normed2 = norm_rows(middle, gains[l][1]).astype(bf16)
            normed2 = ring.gather(normed2).reshape(n * row_count, D)
            gate_up = dot(normed2, in_proj[l])
            gate, up = gate_up[:, :unit_pad], gate_up[:, unit_pad:]
            activated = (jax.nn.silu(gate) * up).astype(bf16)[:, :units]
            terms = dot(activated, down_proj[l]).astype(bf16)
            after = middle + ring.reduce(terms.reshape(n, row_count, D))
            return after, (normed2, gate, up, activated)

        def mlp_backward(gradient, grad_low, middle, stored, l):
            normed2, gate, up, activated = stored
            act_grad = dot_cols(grad_low, down_proj[l])
            act_grad = jnp.pad(act_grad, ((0, 0), (0, unit_pad - units)))
            unused, unit_back = jax.vjp(lambda g, u: jax.nn.silu(g) * u, gate, up)
            gate_grad, up_grad = unit_back(act_grad)
            gate_up_grad = jnp.concatenate([gate_grad.astype(bf16), up_grad.astype(bf16)], axis=1)
            terms = dot_cols(gate_up_grad, in_proj[l]).astype(bf16)
            normed_grad = ring.reduce(terms.reshape(n, row_count, D))
            in_part = feed_in_terms(dot_rows(normed2, gate_up_grad))
            down_part = lax.psum_scatter(
                dot_rows(activated, grad_low).astype(bf16), "wt", scatter_dimension=0, tiled=True
            )
            unused, norm_back = jax.vjp(norm_rows, middle, gains[l][1])
            middle_part, gain_grad = norm_back(normed_grad)
            return gradient + middle_part, gain_grad, in_part, down_part.astype(f32)

        def attention_backward(gradient, hidden, stored, mlp_gain_term, l):
            normed_rel, queries, all_keys, all_values, row_max, row_sum, heads_rel = stored
            score_scale = HEAD ** (-0.5)
            grad_low = gradient.astype(bf16)
            out_part = reduce_rows(dot_rows(heads_rel, grad_low))
            heads_grad = from_rel(dot_cols(grad_low, out_proj[l]).astype(bf16)).astype(bf16)
            heads_grad = heads_grad.reshape(row_count, KV_HEADS, HEADS // KV_HEADS, HEAD)
            grouped, scores = grouped_scores(queries, all_keys)
            attn_probs = jnp.exp(scores - row_max) / row_sum
            prob_grad = jnp.einsum(
                "tkgd,skd->tkgs", heads_grad, all_values, preferred_element_type=f32
            )
            row_inner = jnp.sum(attn_probs * prob_grad, axis=-1, keepdims=True)
            score_grad = (attn_probs * (prob_grad - row_inner)).astype(bf16)
            key_terms = (
                jnp.einsum("tkgs,tkgd->skd", score_grad, grouped, preferred_element_type=f32)
                * score_scale
            )
            value_terms = jnp.einsum(
                "tkgs,tkgd->skd", attn_probs.astype(bf16), heads_grad, preferred_element_type=f32
            )
            kv_terms = jnp.stack([key_terms, value_terms], axis=1).astype(bf16)
            kv_grad = ring.reduce(kv_terms.reshape(n, row_count, 2 * KV_W))
            query_grad = jnp.einsum(
                "tkgs,skd->tkgd", score_grad, all_keys, preferred_element_type=f32
            )
            query_grad = query_grad.reshape(row_count, HEADS, HEAD) * score_scale

            def turn(tensor):
                return rotate(tensor, cos_table, sin_table)

            unused, query_back = jax.vjp(turn, query_grad)
            query_part = query_back(query_grad)[0].reshape(row_count, QW).astype(bf16)
            own_key_grad = kv_grad[:, :KV_W].reshape(row_count, KV_HEADS, HEAD)
            unused, key_back = jax.vjp(turn, own_key_grad)
            key_part = key_back(own_key_grad)[0].reshape(row_count, KV_W)
            kv_part = jnp.concatenate([key_part, kv_grad[:, KV_W:]], axis=1).astype(bf16)

            query_sums = reduce_rows(dot_rows(normed_rel, query_part))
            rel_grad = dot_cols(query_part, joint[l][:, :QW]) + dot_cols(
                kv_part, joint[l][:, QW:]
            )
            rel_high = rel_grad.astype(bf16)
            rel_low = (rel_grad - rel_high.astype(f32)).astype(bf16)
            normed_grad = from_rel(rel_high) + from_rel(rel_low)
            unused, norm_back = jax.vjp(norm_rows, hidden, gains[l][0])
            hidden_part, gain_grad = norm_back(normed_grad)
            gain_terms = jnp.pad(
                jnp.stack([gain_grad, mlp_gain_term]).astype(bf16), ((0, 126), (0, 0))
            )
            last_terms = jnp.concatenate(
                [dot_rows(normed_rel, kv_part), lax.dot_general(
                    perm, gain_terms, (((0,), (1,)), ((), ())), preferred_element_type=f32
                )], axis=1
            )
            last_sums = reduce_rows(last_terms)
            joint_part = jnp.concatenate([query_sums, last_sums[:, : 2 * KV_W]], axis=1)
            bias_part = lax.dynamic_slice(joint_part, (rows, shard * bias_w), (1, bias_w))[0]
            attn_gain_part = last_sums[:rows, 2 * KV_W]
            mlp_gain_part = last_sums[:rows, 2 * KV_W + 1]
            return gradient + hidden_part, (
                attn_gain_part,
                joint_part[:rows],
                bias_part,
                out_part[:rows],
                mlp_gain_part,
            )

        hidden = hidden_in[0].astype(f32)
        stored_layers = []
        for l in range(LAYERS):
            middle, attn_stored = attention_forward(hidden, l)
            after, mlp_stored = mlp_forward(middle, l)
            stored_layers.append((hidden, attn_stored, middle, mlp_stored))
            hidden = after
        gradient = cotangent[0].astype(f32)
        grad_low = cotangent_low
        attn_sums, in_sums, down_sums = [None] * LAYERS, [None] * LAYERS, [None] * LAYERS
        for l in reversed(range(LAYERS)):
            layer_input, attn_stored, middle, mlp_stored = stored_layers[l]
            if grad_low is None:
                grad_low = ring.gather(gradient.astype(bf16)).reshape(n * row_count, D)
            gradient, mlp_gain_term, in_sums[l], down_sums[l] = mlp_backward(
                gradient, grad_low, middle, mlp_stored, l
            )
            gradient, attn_sums[l] = attention_backward(
                gradient, layer_input, attn_stored, mlp_gain_term, l
            )
            grad_low = None
        in_weight_grad = feed_in_home(in_sums)
        stacked = [jnp.stack([part[i] for part in attn_sums]) for i in range(5)]
        return (
            hidden[None],
            gradient[None],
            *stacked,
            in_weight_grad,
            jnp.stack(down_sums),
        )

    return body


def solution(mesh):
    shape = dict(mesh.shape)
    return jax.shard_map(
        make_body(shape["ctx"], shape["wt"]),
        mesh=mesh,
        in_specs=(
            P("wt", "ctx", None),
            P("wt", "ctx"),
            P("wt", "ctx", None),
            P(None, ("ctx", "wt")),
            P(None, ("ctx", "wt"), None),
            P(None, ("ctx", "wt")),
            P(None, ("ctx", "wt"), None),
            P(None, ("ctx", "wt")),
            P(None, ("ctx", "wt"), None),
            P(None, ("ctx", "wt"), None),
        ),
        out_specs=(
            P("wt", "ctx", None),
            P("wt", "ctx", None),
            P(None, ("ctx", "wt")),
            P(None, ("ctx", "wt"), None),
            P(None, ("ctx", "wt")),
            P(None, ("ctx", "wt"), None),
            P(None, ("ctx", "wt")),
            P(None, ("ctx", "wt"), None),
            P(None, ("ctx", "wt"), None),
        ),
        check_vma=False,
    )
```

```python
import functools
import math

import jax
import jax.numpy as jnp
from jax import lax
from jax.experimental import pallas as pl
from jax.experimental.pallas import tpu as pltpu
from jax.sharding import PartitionSpec as P

HEADS = 14
KV_HEADS = 2
GROUP = HEADS // KV_HEADS
HEAD = 64
FF = 4864
LAYERS = 2
QW = 896
D = 896
QKV_W = 1152
KV_W = KV_HEADS * HEAD

EPSILON = 1e-06
ROPE_BASE = 1000000.0
NEGATIVE = -1e30
SCALE = HEAD**-0.5

bf16 = jnp.bfloat16
f32 = jnp.float32

ANY = pl.BlockSpec(memory_space=pl.ANY)
VMEM = pl.BlockSpec(memory_space=pltpu.VMEM)
DMA = pltpu.SemaphoreType.DMA


def shape(dims, dtype):
    return jax.ShapeDtypeStruct(dims, dtype)


def dot(left, right):
    return jnp.dot(left, right, preferred_element_type=f32)


def dot_rows(left, right):
    return lax.dot_general(left, right, (((0,), (0,)), ((), ())), preferred_element_type=f32)


def dot_cols(left, right):
    return lax.dot_general(left, right, (((1,), (1,)), ((), ())), preferred_element_type=f32)


def run(kernel, ins, in_specs, outs, out_specs, scratch, flops, vmem=60):
    moved = sum(math.prod(x.shape) * x.dtype.itemsize for x in [*ins, *outs])
    return pl.pallas_call(
        kernel,
        out_shape=outs,
        in_specs=in_specs,
        out_specs=out_specs,
        scratch_shapes=scratch,
        compiler_params=pltpu.CompilerParams(vmem_limit_bytes=vmem * 2**20),
        cost_estimate=pl.CostEstimate(flops=flops, bytes_accessed=moved, transcendentals=0),
    )(*ins)


def copies(sources, targets, sems):
    made = [pltpu.make_async_copy(s, t, sems.at[i]) for i, (s, t) in enumerate(zip(sources, targets))]
    for c in made:
        c.start()
    return made


def rows_of(ref, count, size):
    return [ref.at[pl.ds(i * size, size)] for i in range(count)]


class Blocks:
    def __init__(self, arrays, places):
        self.arrays, self.places = arrays, places

    def take(self, it):
        refs = [next(it) for _ in self.arrays]
        return [refs[a].at[b] for a, b in self.places]


def turned(block):
    lane = lax.broadcasted_iota(jnp.int32, block.shape, 1)
    return jnp.where(lane % HEAD < HEAD // 2, -pltpu.roll(block, 96, 1), pltpu.roll(block, 32, 1))


def rotated(block, cos, sin):
    return block * cos + turned(block) * sin


def rotated_back(block, cos, sin):
    return block * cos - turned(block) * sin


def inverse_norm(hidden):
    return lax.rsqrt(jnp.mean(hidden * hidden, axis=-1, keepdims=True) + EPSILON)


def norm_back(normed_grad, hidden, gain):
    inverse = inverse_norm(hidden)
    scaled = normed_grad * gain
    inner = jnp.mean(scaled * hidden, axis=-1, keepdims=True)
    into = inverse * scaled - hidden * (inverse * inverse * inverse * inner)
    return into, jnp.sum(normed_grad * (hidden * inverse), axis=0, keepdims=True)


def split_dot_cols(value, right):
    high = value.astype(bf16)
    low = (value - high.astype(f32)).astype(bf16)
    return dot_cols(high, right) + dot_cols(low, right)


def first_row(row):
    return jnp.broadcast_to(row, (8, row.shape[1]))


def before_attention(cfg, base, sums, perm, cos, sin, blocks, places=None):
    n, m, rows, pad_rows = cfg
    tokens, step = base.shape[0], m * pad_rows
    all_rows = n * step
    more = [] if places is None else [places]

    def kernel(*refs):
        it = iter(refs)
        more_refs = [next(it) for _ in more]
        base_ref = next(it)
        sum_refs = [next(it) for _ in sums]
        perm_ref, cos_ref, sin_ref = next(it), next(it), next(it)
        block_refs = blocks.take(it)
        hidden_ref, rel_ref, query_ref, kv_ref, gain_ref, weight, sems = it
        waits = copies(
            [b.at[:, pl.ds(0, QKV_W)] for b in block_refs], rows_of(weight, n, step), sems
        )
        hidden = base_ref[...].astype(f32)
        for ref in sum_refs:
            hidden = hidden + ref[...].astype(f32)
        hidden_ref[...] = hidden
        scaled = hidden * inverse_norm(hidden)
        cos, sin = cos_ref[...], sin_ref[...]
        for w in waits:
            w.wait()
        last = jnp.zeros((16, QKV_W), f32)
        for i in range(n * m):
            last = last + weight[pl.ds((i + 1) * pad_rows - 16, 16), :].astype(f32)
        at = rows + 1 - (pad_rows - 16)
        gain_ref[0:8, :] = first_row(last[at : at + 1, :D])
        gain_ref[8:16, :] = first_row(last[at + 1 : at + 2, :D])
        normed = (scaled * last[at : at + 1, :D]).astype(bf16)
        rel = dot(normed, perm_ref[...])
        lane = lax.broadcasted_iota(jnp.int32, rel.shape, 1)
        rel = jnp.where(lane % pad_rows == rows, 1.0, rel).astype(bf16)
        rel_ref[...] = rel
        kv = dot(rel, weight[:, QW:])
        kv_ref[:, :KV_W] = rotated(kv[:, :KV_W], cos, sin).astype(bf16)
        kv_ref[:, KV_W : 2 * KV_W] = kv[:, KV_W:].astype(bf16)
        for ref in more_refs:
            kv_ref[:, 2 * KV_W :] = ref[...]
        query = dot(rel, weight[:, :QW])
        for i in range(QW // 128):
            part = rotated(query[:, i * 128 : (i + 1) * 128], cos, sin).astype(bf16)
            query_ref[:, i * 128 : (i + 1) * 128] = part * SCALE

    ins = [*more, base, *sums, perm, cos, sin]
    return run(
        kernel,
        [*ins, *blocks.arrays],
        [VMEM] * len(ins) + [ANY] * len(blocks.arrays),
        [
            shape((tokens, D), f32),
            shape((tokens, all_rows), bf16),
            shape((tokens, QW), bf16),
            shape((tokens, 2 * KV_W + 128 * len(more)), bf16),
            shape((16, D), f32),
        ],
        [VMEM] * 5,
        [pltpu.VMEM((all_rows, QKV_W), bf16), DMA((n,))],
        2 * tokens * all_rows * (D + QKV_W),
    )


def kv_copies(n, tokens, kv_refs, place_refs, kv, place, sems):
    return copies(
        [
            *[r.at[:, pl.ds(0, 2 * KV_W)] for r in kv_refs],
            *[r.at[:, pl.ds(2 * KV_W, 128)] for r in place_refs],
        ],
        [*rows_of(kv, n, tokens), *rows_of(place, n, tokens)],
        sems,
    )


def place_column(place, at):
    block = place[at, :].astype(f32)
    return (block[:, 0:1] * 256.0 + block[:, 1:2]).astype(jnp.int32)


def heads_to_lanes(matrix, group, tokens):
    parts = [
        matrix[(group * GROUP + h) * HEAD : (group * GROUP + h + 1) * HEAD, :] for h in range(GROUP)
    ]
    return jnp.concatenate(parts, axis=1)


def lanes_to_heads(groups, tokens):
    parts = [g[:, h * tokens : (h + 1) * tokens] for g in groups for h in range(GROUP)]
    return jnp.concatenate(parts, axis=0).T


def heads_to_rows(matrix, group):
    parts = [
        matrix[:, (group * GROUP + h) * HEAD : (group * GROUP + h + 1) * HEAD] for h in range(GROUP)
    ]
    return jnp.concatenate(parts, axis=0)


def attention(
    cfg, query, kv_blocks, own_row, place_blocks, hidden, gain, perm, perm2, out_blocks, out_at
):
    n, m, rows, pad_rows = cfg
    tokens, step = query.shape[0], m * pad_rows
    all_rows, wide = n * step, GROUP * query.shape[0]
    slots = KV_HEADS if n <= 8 else 1

    def kernel(*refs):
        it = iter(refs)
        query_ref = next(it)
        kv_refs = [next(it) for _ in range(n)]
        place_refs = [next(it) for _ in range(n)]
        row_ref, hidden_ref, gain_ref, perm_in, perm2_in = [next(it) for _ in range(5)]
        out_refs = out_blocks.take(it)
        middle_ref, normed_ref, rel_ref, mix_ref, lse_ref, turn_ref = [next(it) for _ in range(6)]
        kv, place, values_t, scores = [next(it) for _ in range(4)]
        probs = next(it) if slots > 1 else None
        perm_v, perm2_v, weight, kv_sems, sems = it
        kv_waits = kv_copies(n, tokens, kv_refs, place_refs, kv, place, kv_sems)
        waits = copies(
            [perm_in, perm2_in, *[o.at[:, pl.ds(out_at, D)] for o in out_refs]],
            [perm_v, perm2_v, *rows_of(weight, n, step)],
            sems,
        )
        query_t = query_ref[...].astype(f32).T
        for w in kv_waits:
            w.wait()
        for g in range(KV_HEADS):
            turn_ref[g * HEAD : (g + 1) * HEAD, :] = heads_to_lanes(query_t, g, tokens).astype(bf16)

        if probs is None:
            for j in range(n):
                block = kv[pl.ds(j * tokens, tokens), KV_W:]
                values_t[j] = block.astype(f32).T.astype(bf16)
        else:
            values_t[...] = kv[:, KV_W:].astype(f32).T.astype(bf16)
        own = row_ref[...]
        mixed = []
        for g in range(KV_HEADS):
            turn = turn_ref[g * HEAD : (g + 1) * HEAD, :]
            top = jnp.full((1, wide), NEGATIVE, f32)
            for j in range(n):
                at = pl.ds(j * tokens, tokens)
                s = dot(kv[at, g * HEAD : (g + 1) * HEAD], turn)
                s = jnp.where(place_column(place, at) <= own, s, NEGATIVE)
                scores[g % slots, at, :] = s
                top = jnp.maximum(top, jnp.max(s, axis=0, keepdims=True))
            total = jnp.zeros((1, wide), f32)
            out = jnp.zeros((HEAD, wide), f32)
            for j in range(n):
                at = pl.ds(j * tokens, tokens)
                p = jnp.exp(scores[g % slots, at, :] - top)
                total = total + jnp.sum(p, axis=0, keepdims=True)
                if probs is None:
                    out = out + dot(values_t[j, g * HEAD : (g + 1) * HEAD, :], p.astype(bf16))
                else:
                    probs[g, at, :] = p.astype(bf16)
            if probs is not None:
                out = dot(values_t[g * HEAD : (g + 1) * HEAD, :], probs[g])
            out = out / total
            mix_ref[g * HEAD : (g + 1) * HEAD, :] = out
            lse_ref[g * 8 : (g + 1) * 8, :] = first_row(top + jnp.log(total))
            mixed.append(out)
        heads = lanes_to_heads(mixed, tokens).astype(bf16)
        for w in waits:
            w.wait()
        rel = dot(heads, perm_v[...]).astype(bf16)
        rel_ref[...] = rel
        middle = hidden_ref[...] + dot(rel, weight[...])
        middle_ref[...] = middle
        normed = (middle * inverse_norm(middle) * gain_ref[8:9, :]).astype(bf16)
        normed_ref[...] = dot(normed, perm2_v[...]).astype(bf16)

    return run(
        kernel,
        [query, *kv_blocks, *place_blocks, own_row, hidden, gain, perm, perm2, *out_blocks.arrays],
        [VMEM] + [ANY] * (2 * n) + [VMEM] * 3 + [ANY] * (len(out_blocks.arrays) + 2),
        [
            shape((tokens, D), f32),
            shape((tokens, D), bf16),
            shape((tokens, all_rows), bf16),
            shape((KV_W, wide), f32),
            shape((16, wide), f32),
            shape((KV_W, wide), bf16),
        ],
        [VMEM] * 6,
        [
            pltpu.VMEM((n * tokens, 2 * KV_W), bf16),
            pltpu.VMEM((n * tokens, 128), bf16),
            pltpu.VMEM((KV_W, n * tokens) if slots > 1 else (n, KV_W, tokens), bf16),
            pltpu.VMEM((slots, n * tokens, wide), f32),
            *([pltpu.VMEM((slots, n * tokens, wide), bf16)] if slots > 1 else []),
            pltpu.VMEM((D, all_rows), bf16),
            pltpu.VMEM((D, D), bf16),
            pltpu.VMEM((all_rows, D), bf16),
            DMA((2 * n,)),
            DMA((n + 2,)),
        ],
        8 * tokens * n * tokens * QW,
        60,
    )


def middle_back(cfg, sums, middle, gradient, gain, perm, perm2, out_blocks, out_at):
    n, m, rows, pad_rows = cfg
    tokens, step = middle.shape[0], m * pad_rows
    all_rows = n * step

    def kernel(*refs):
        it = iter(refs)
        sum_refs = [next(it), next(it)]
        middle_ref, grad_ref, gain_ref, perm_in, perm2_ref = [next(it) for _ in range(5)]
        out_refs = out_blocks.take(it)
        mgrad_ref, low_ref, gain_grad_ref, heads_ref = [next(it) for _ in range(4)]
        perm_v, weight, sems = it
        waits = copies(
            [perm_in, *[o.at[:, pl.ds(out_at, D)] for o in out_refs]],
            [perm_v, *rows_of(weight, n, step)],
            sems,
        )
        normed_grad = split_dot_cols(
            sum_refs[0][...] + sum_refs[1][...].astype(f32), perm2_ref[...]
        )
        into, gain_grad = norm_back(normed_grad, middle_ref[...], gain_ref[8:9, :])
        middle_grad = grad_ref[...].astype(f32) + into
        mgrad_ref[...] = middle_grad
        gain_grad_ref[...] = first_row(gain_grad)
        low = middle_grad.astype(bf16)
        low_ref[...] = low
        for w in waits:
            w.wait()
        heads_rel = dot_cols(low, weight[...]).astype(bf16)
        heads_ref[...] = dot_cols(heads_rel, perm_v[...]).astype(bf16)

    return run(
        kernel,
        [*sums, middle, gradient, gain, perm, perm2, *out_blocks.arrays],
        [VMEM] * 5 + [ANY] + [VMEM] + [ANY] * len(out_blocks.arrays),
        [
            shape((tokens, D), f32),
            shape((tokens, D), bf16),
            shape((8, D), f32),
            shape((tokens, QW), bf16),
        ],
        [VMEM] * 4,
        [pltpu.VMEM((D, all_rows), bf16), pltpu.VMEM((all_rows, D), bf16), DMA((n + 1,))],
        2 * tokens * D * (2 * D + 2 * all_rows),
    )


def attention_back(
    cfg, heads_grad, mix, lse, turn, query, kv_blocks, own_row, place_blocks, cos, sin
):
    n, m, rows, pad_rows = cfg
    tokens, half = query.shape[0], n // 2
    wide = GROUP * query.shape[0]

    def kernel(*refs):
        it = iter(refs)
        heads_ref, mix_ref, lse_ref, turn_ref, query_ref = [next(it) for _ in range(5)]
        kv_refs = [next(it) for _ in range(n)]
        place_refs = [next(it) for _ in range(n)]
        row_ref, cos_ref, sin_ref = [next(it) for _ in range(3)]
        keep_ref, send_ref, part_ref = [next(it) for _ in range(3)]
        kv, place, keys_t, probs, score_grads, kv_sems = it
        kv_waits = kv_copies(n, tokens, kv_refs, place_refs, kv, place, kv_sems)
        heads = heads_ref[...]
        heads_t = heads.astype(f32).T
        for w in kv_waits:
            w.wait()
        keys_t[...] = kv[:, :KV_W].astype(f32).T.astype(bf16)
        own = row_ref[...]
        query = query_ref[...]
        sides = []
        for g in range(KV_HEADS):
            grad_t = heads_to_lanes(heads_t, g, tokens)
            inner = jnp.sum(mix_ref[g * HEAD : (g + 1) * HEAD, :] * grad_t, axis=0, keepdims=True)
            sides.append(
                (
                    turn_ref[g * HEAD : (g + 1) * HEAD, :],
                    heads_to_rows(query, g),
                    grad_t.astype(bf16),
                    heads_to_rows(heads, g),
                    inner,
                    lse_ref[g * 8 : g * 8 + 1, :],
                )
            )
        wholes = []
        for g, (turn, query_rows, grad_t, grad_rows, inner, lse) in enumerate(sides):
            for j in range(n):
                at = pl.ds(j * tokens, tokens)
                s = dot(kv[at, g * HEAD : (g + 1) * HEAD], turn)
                p = jnp.exp(jnp.where(place_column(place, at) <= own, s, NEGATIVE) - lse)
                prob_grad = dot(kv[at, KV_W + g * HEAD : KV_W + (g + 1) * HEAD], grad_t)
                probs[at, :] = p.astype(bf16)
                score_grads[at, :] = (p * (prob_grad - inner)).astype(bf16)
            for part, ref in enumerate([keep_ref, send_ref]):
                at = pl.ds(part * half * tokens, half * tokens)
                key_out = dot(score_grads[at, :], query_rows).astype(bf16)
                value_out = dot(probs[at, :], grad_rows).astype(bf16)
                ref[:, g * HEAD : (g + 1) * HEAD] = key_out
                ref[:, KV_W + g * HEAD : KV_W + (g + 1) * HEAD] = value_out
            wholes.append(dot(keys_t[g * HEAD : (g + 1) * HEAD, :], score_grads[...]))
        whole = lanes_to_heads(wholes, tokens) * SCALE
        cos, sin = cos_ref[...], sin_ref[...]
        for i in range(QW // 128):
            at = slice(i * 128, (i + 1) * 128)
            part_ref[:, at] = rotated_back(whole[:, at], cos, sin).astype(bf16)

    return run(
        kernel,
        [heads_grad, mix, lse, turn, query, *kv_blocks, *place_blocks, own_row, cos, sin],
        [VMEM] * 5 + [ANY] * (2 * n) + [VMEM] * 3,
        [
            shape((half * tokens, 2 * KV_W), bf16),
            shape((half * tokens, 2 * KV_W), bf16),
            shape((tokens, QW), bf16),
        ],
        [VMEM] * 3,
        [
            pltpu.VMEM((n * tokens, 2 * KV_W), bf16),
            pltpu.VMEM((n * tokens, 128), bf16),
            pltpu.VMEM((KV_W, n * tokens), bf16),
            pltpu.VMEM((n * tokens, wide), bf16),
            pltpu.VMEM((n * tokens, wide), bf16),
            DMA((2 * n,)),
        ],
        20 * tokens * n * tokens * QW,
        60,
    )


def query_back(cfg, query_part, blocks):
    n, m, rows, pad_rows = cfg
    tokens, step = query_part.shape[0], m * pad_rows

    def kernel(*refs):
        it = iter(refs)
        part_ref, block_refs = next(it), blocks.take(it)
        out_ref, weight, sems = it
        waits = copies(
            [b.at[:, pl.ds(0, QW)] for b in block_refs], rows_of(weight, n, step), sems
        )
        for w in waits:
            w.wait()
        out_ref[...] = dot_cols(part_ref[...], weight[...])

    return run(
        kernel,
        [query_part, *blocks.arrays],
        [VMEM] + [ANY] * len(blocks.arrays),
        [shape((tokens, n * step), f32)],
        [VMEM],
        [pltpu.VMEM((n * step, QW), bf16), DMA((n,))],
        2 * tokens * n * step * QW,
    )[0]


def layer_back(cfg, sums, query_rel, hidden, middle_grad, gain, cos, sin, perm, blocks):
    n, m, rows, pad_rows = cfg
    tokens, step = hidden.shape[0], m * pad_rows

    def kernel(*refs):
        it = iter(refs)
        sum_refs = [next(it), next(it)]
        rel_ref, hidden_ref, mgrad_ref, gain_ref, cos_ref, sin_ref, perm_ref = [
            next(it) for _ in range(7)
        ]
        block_refs = blocks.take(it)
        grad_ref, low_ref, part_ref, gain_grad_ref, weight, sems = it
        waits = copies(
            [b.at[:, pl.ds(QW, 2 * KV_W)] for b in block_refs], rows_of(weight, n, step), sems
        )
        total = sum_refs[0][...] + sum_refs[1][...].astype(f32)
        keys = rotated_back(total[:, :KV_W], cos_ref[...], sin_ref[...])
        part = jnp.concatenate([keys, total[:, KV_W:]], axis=1).astype(bf16)
        part_ref[...] = part
        for w in waits:
            w.wait()
        rel = rel_ref[...] + dot_cols(part, weight[...])
        normed_grad = split_dot_cols(rel, perm_ref[...])
        into, gain_grad = norm_back(normed_grad, hidden_ref[...], gain_ref[0:1, :])
        gradient = mgrad_ref[...] + into
        grad_ref[...] = gradient
        low_ref[...] = gradient.astype(bf16)
        gain_grad_ref[...] = first_row(gain_grad)

    return run(
        kernel,
        [*sums, query_rel, hidden, middle_grad, gain, cos, sin, perm, *blocks.arrays],
        [VMEM] * 9 + [ANY] * len(blocks.arrays),
        [
            shape((tokens, D), f32),
            shape((tokens, D), bf16),
            shape((tokens, 2 * KV_W), bf16),
            shape((8, D), f32),
        ],
        [VMEM] * 4,
        [pltpu.VMEM((n * step, 2 * KV_W), bf16), DMA((n,))],
        2 * tokens * n * step * (2 * KV_W + 2 * D),
    )


def gated(gate, up):
    return gate * jax.nn.sigmoid(gate) * up


def gated_back(act_grad, gate, up):
    sig = jax.nn.sigmoid(gate)
    gate_grad = act_grad * up * (sig * (1.0 + gate * (1.0 - sig)))
    return gate_grad, act_grad * (gate * sig)


def feed_forward(x_blocks, in_proj, down_proj):
    n, tokens, units, width = len(x_blocks), x_blocks[0].shape[0], down_proj.shape[0], in_proj.shape[1]
    half, pad, total = n // 2, width // 2, n * tokens

    def kernel(*refs):
        x_refs, (in_ref, down_ref) = refs[:n], refs[n : n + 2]
        keep_ref, send_ref, all_ref, unit_ref, act_ref = refs[n + 2 : n + 7]
        x, w_in, w_down, units_v, act_v, terms, x_sems, w_sems, o_sems = refs[n + 7 :]
        in_wait, down_wait = copies([in_ref, down_ref], [w_in, w_down.at[pl.ds(0, units)]], w_sems)
        x_waits = copies(x_refs, rows_of(x, n, tokens), x_sems)
        if pad > units:
            w_down[units:, :] = jnp.zeros((pad - units, D), bf16)
        in_wait.wait()
        down_wait.wait()
        outs = []

        def put(src, dst, slot):
            copy = pltpu.make_async_copy(src, dst, o_sems.at[slot])
            copy.start()
            outs.append(copy)

        big = half * tokens
        for i, (part, target) in enumerate([(1, send_ref), (0, keep_ref)]):
            at = pl.ds(part * big, big)
            for w in x_waits[part * half : (part + 1) * half]:
                w.wait()
            put(x.at[at], all_ref.at[at], 4 * i)
            both = dot(x[at, :], w_in[...])
            units_v[at, :] = both.astype(bf16)
            put(units_v.at[at], unit_ref.at[at], 4 * i + 1)
            act = gated(both[:, :pad], both[:, pad:]).astype(bf16)
            act_v[at, :] = act
            put(act_v.at[at], act_ref.at[at], 4 * i + 2)
            terms[part] = dot(act, w_down[...]).astype(bf16)
            put(terms.at[part], target, 4 * i + 3)
        for copy in outs:
            copy.wait()

    return run(
        kernel,
        [*x_blocks, in_proj, down_proj],
        [ANY] * (n + 2),
        [
            shape((half * tokens, D), bf16),
            shape((half * tokens, D), bf16),
            shape((total, D), bf16),
            shape((total, width), bf16),
            shape((total, pad), bf16),
        ],
        [ANY] * 5,
        [
            pltpu.VMEM((total, D), bf16),
            pltpu.VMEM((D, width), bf16),
            pltpu.VMEM((pad, D), bf16),
            pltpu.VMEM((total, width), bf16),
            pltpu.VMEM((total, pad), bf16),
            pltpu.VMEM((2, half * tokens, D), bf16),
            DMA((n,)),
            DMA((2,)),
            DMA((8,)),
        ],
        2 * total * D * (width + pad),
        60,
    )


def feed_forward_back(x_blocks, units_all, grad_blocks, in_proj, down_proj):
    n, tokens = len(grad_blocks), grad_blocks[0].shape[0]
    units, width = down_proj.shape[0], in_proj.shape[1]
    half, pad, total = n // 2, width // 2, n * tokens
    fresh = units_all is None

    def kernel(*refs):
        it = iter(refs)
        x_refs = [next(it) for _ in range(n)] if fresh else []
        unit_ref = None if fresh else next(it)
        g_refs = [next(it) for _ in range(n)]
        in_ref, down_ref = next(it), next(it)
        keep_ref, send_ref, gall_ref, ugrad_ref = [next(it) for _ in range(4)]
        all_ref, act_ref = (next(it), next(it)) if fresh else (None, None)
        g, w_in, w_down, ugrad, terms = [next(it) for _ in range(5)]
        x, act_v = (next(it), next(it)) if fresh else (None, None)
        units_v = None if fresh else next(it)
        g_sems, w_sems, o_sems, x_sems = it
        in_wait, down_wait = copies([in_ref, down_ref], [w_in, w_down.at[pl.ds(0, units)]], w_sems)
        g_waits = copies(g_refs, rows_of(g, n, tokens), g_sems)
        if fresh:
            x_waits = copies(x_refs, rows_of(x, n, tokens), x_sems)
        else:
            x_waits = copies(rows_of(unit_ref, n, tokens), rows_of(units_v, n, tokens), x_sems)
        if pad > units:
            w_down[units:, :] = jnp.zeros((pad - units, D), bf16)
        in_wait.wait()
        down_wait.wait()
        outs = []

        def put(src, dst, slot):
            copy = pltpu.make_async_copy(src, dst, o_sems.at[slot])
            copy.start()
            outs.append(copy)

        big = half * tokens
        for i, (part, target) in enumerate([(1, send_ref), (0, keep_ref)]):
            at = pl.ds(part * big, big)
            for w in x_waits[part * half : (part + 1) * half]:
                w.wait()
            if fresh:
                put(x.at[at], all_ref.at[at], 5 * i)
                both = dot(x[at, :], w_in[...])
                gate, up = both[:, :pad], both[:, pad:]
                act_v[at, :] = gated(gate, up).astype(bf16)
                put(act_v.at[at], act_ref.at[at], 5 * i + 1)
            else:
                gate, up = units_v[at, :pad].astype(f32), units_v[at, pad:].astype(f32)
            for w in g_waits[part * half : (part + 1) * half]:
                w.wait()
            put(g.at[at], gall_ref.at[at], 5 * i + 2)
            gate_grad, up_grad = gated_back(dot_cols(g[at, :], w_down[...]), gate, up)
            ugrad[at, :pad] = gate_grad.astype(bf16)
            ugrad[at, pad:] = up_grad.astype(bf16)
            put(ugrad.at[at], ugrad_ref.at[at], 5 * i + 3)
            terms[part] = dot_cols(ugrad[at, :], w_in[...]).astype(bf16)
            put(terms.at[part], target, 5 * i + 4)
        for copy in outs:
            copy.wait()

    ins = [*(x_blocks if fresh else [units_all]), *grad_blocks, in_proj, down_proj]
    outs = [
        shape((half * tokens, D), bf16),
        shape((half * tokens, D), bf16),
        shape((total, D), bf16),
        shape((total, width), bf16),
    ]
    scratch = [
        pltpu.VMEM((total, D), bf16),
        pltpu.VMEM((D, width), bf16),
        pltpu.VMEM((pad, D), bf16),
        pltpu.VMEM((total, width), bf16),
        pltpu.VMEM((2, half * tokens, D), bf16),
    ]
    if fresh:
        outs += [shape((total, D), bf16), shape((total, pad), bf16)]
        scratch += [pltpu.VMEM((total, D), bf16), pltpu.VMEM((total, pad), bf16)]
    else:
        scratch += [pltpu.VMEM((total, width), bf16)]
    scratch += [DMA((n,)), DMA((2,)), DMA((10,)), DMA((n,))]
    return run(
        kernel,
        ins,
        [ANY] * len(ins),
        outs,
        [ANY] * len(outs),
        scratch,
        2 * total * D * (width * (2 if fresh else 1) + pad),
        60,
    )


def cut_columns(order, weights, units, unit_pad):
    n, (rows, _), layers = order.shape[0], weights[0].shape, len(weights)

    def kernel(order_ref, *refs):
        weight_refs, outs, parts = refs[:layers], refs[layers:-1], refs[-1]
        zeros = jnp.zeros((rows, unit_pad - units), bf16)
        for l in range(layers):
            for c in range(n):
                for k in range(2):
                    at, to = k * FF + c * units, k * unit_pad
                    parts[c, l, :, to : to + units] = weight_refs[l][:, at : at + units]
                    if unit_pad > units:
                        parts[c, l, :, to + units : to + unit_pad] = zeros
        for a in range(n):
            outs[a][...] = parts[order_ref[a]]

    return run(
        kernel,
        [order, *weights],
        [pl.BlockSpec(memory_space=pltpu.SMEM)] + [VMEM] * layers,
        [shape((layers, rows, 2 * unit_pad), bf16)] * n,
        [VMEM] * n,
        [pltpu.VMEM((n, layers, rows, 2 * unit_pad), bf16)],
        0,
    )


def join_rows(order, blocks):
    n, (layers, rows, width) = len(blocks), blocks[0].shape

    def kernel(order_ref, *refs):
        block_refs, outs, parts = refs[:n], refs[n:-1], refs[-1]
        for a in range(n):
            parts[order_ref[a]] = block_refs[a][...]
        for l in range(layers):
            for c in range(n):
                outs[l][c * rows : (c + 1) * rows, :] = parts[c, l]

    return run(
        kernel,
        [order, *blocks],
        [pl.BlockSpec(memory_space=pltpu.SMEM)] + [VMEM] * n,
        [shape((n * rows, width), bf16)] * layers,
        [VMEM] * layers,
        [pltpu.VMEM((n, layers, rows, width), bf16)],
        0,
    )


class Ring:
    def __init__(self, n, m):
        self.n, self.m = n, m
        if n == 8:
            self.even = [0, 4, 2, 6, 1, 3, 5, 7]
            self.odd = [0, 2, 4, 6, 1, 5, 3, 7]
        else:
            self.even = self.odd = list(range(n))

    def swap(self, value, offset, odd_offset=None):
        odd_offset = offset if odd_offset is None else odd_offset
        return lax.ppermute(
            value, "ctx", [(i, i ^ (odd_offset if i % 2 else offset)) for i in range(self.n)]
        )

    def swap_z(self, value, offset):
        return lax.ppermute(value, "wt", [(i, i ^ offset) for i in range(self.m)])

    def offsets(self, me):
        return jnp.where(
            me % 2 == 1, jnp.array(self.odd, jnp.int32), jnp.array(self.even, jnp.int32)
        )

    def gather(self, own, *behind):
        if self.n == 8:
            blocks = [own, self.swap(own, 4, 2), self.swap(own, 2, 4), self.swap(own, 6)]
            if behind:
                blocks = [held(b, *behind) for b in blocks]
            return blocks + [self.swap(b, 1) for b in blocks]
        blocks = own[None]
        step = 1
        while step < self.n:
            blocks = jnp.concatenate([blocks, self.swap(blocks, step)])
            step *= 2
        return [blocks[i] for i in range(self.n)]

    def gather_steps(self, own):
        own = own[None]
        if self.n == 8:
            pair = jnp.concatenate([own, self.swap((yield own), 2, 4)])
            pair = yield pair
            other = self.swap(pair, 4, 2)
            other = yield other
            yield Blocks(
                [pair, other, self.swap(pair, 1), self.swap(other, 1)],
                [(0, 0), (1, 0), (0, 1), (1, 1), (2, 0), (3, 0), (2, 1), (3, 1)],
            )
        else:
            blocks, step = own, 1
            count = 0
            while step < self.n:
                if count < 3:
                    blocks = yield blocks
                count += 1
                blocks = jnp.concatenate([blocks, self.swap(blocks, step)])
                step *= 2
            yield Blocks([blocks], [(0, i) for i in range(self.n)])

    def first(self, keep, send):
        count = self.n // 2
        got = self.swap(send, 1 if self.n == 8 else count)
        total = keep.astype(f32) + got.astype(f32)
        return total.reshape(count, -1, keep.shape[-1])

    def outgoing(self, total):
        return total[total.shape[0] // 2 :].astype(bf16)

    def move(self, total, out):
        count = total.shape[0] // 2
        if self.n == 8:
            return self.swap(out, 2, 4) if count == 2 else self.swap(out, 4, 2)
        return self.swap(out, count)

    def add(self, total, got):
        return total[: total.shape[0] // 2] + got.astype(f32)

    def step(self, total):
        return self.add(total, self.move(total, self.outgoing(total)))

    def finish(self, total):
        while total.shape[0] > 2:
            total = self.step(total)
        return total[0], self.move(total, self.outgoing(total))[0]

    def reduce(self, keep, send):
        return self.finish(self.first(keep, send))

    def trade(self, blocks):
        if self.n == 8:
            return [blocks[0]] + [
                self.swap(blocks[i], self.even[i], self.odd[i]) for i in range(1, self.n)
            ]
        return [blocks[0]] + [self.swap(blocks[i], i) for i in range(1, self.n)]

    def sources(self, me):
        even, odd = [0] * self.n, [0] * self.n
        for i in range(self.n):
            even[i] = self.even[i] if self.even[i] % 2 == 0 else self.odd[i]
            odd[i] = self.odd[i] if self.odd[i] % 2 == 0 else self.even[i]
        table = jnp.where(me % 2 == 1, jnp.array(odd, jnp.int32), jnp.array(even, jnp.int32))
        return me ^ table

    def gather_z(self, own):
        return jnp.stack([own] + [self.swap_z(own, k) for k in range(1, self.m)])

    def reduce_z(self, terms):
        total = terms[0].astype(f32)
        for k in range(1, self.m):
            total = total + self.swap_z(terms[k].astype(bf16), k).astype(f32)
        return total


def held(value, *others):
    return lax.optimization_barrier((value, *others))[0]


def make_body(n, m):
    ring = Ring(n, m)
    rows = D // (n * m)
    bias_w = QKV_W // (n * m)
    pad_rows = -(-(rows + 3) // 16) * 16
    step = m * pad_rows
    all_rows = n * step
    units = FF // n
    unit_pad = -(-units // 128) * 128
    cfg = (n, m, rows, pad_rows)

    in_block_row = jnp.arange(all_rows // 2, dtype=jnp.int32)[:, None] % pad_rows

    def row_terms(left, right, *extra_rows):
        cut = all_rows // 2
        halves = []
        for part in (left[:, :cut], left[:, cut:]):
            terms = dot_rows(part, right)
            for i, row in enumerate(extra_rows):
                terms = jnp.where(in_block_row == rows + 1 + i, row, terms)
            halves.append(terms.astype(bf16))
        return halves

    def z_sum(mine, got):
        total = mine + got.astype(f32)
        return ring.reduce_z(total.reshape(m, pad_rows, total.shape[-1]))

    def feed_in_home(parts):
        cut = jnp.stack([p.reshape(n, rows, 2 * unit_pad) for p in parts], axis=1)
        return lax.all_to_all(cut, "ctx", 0, 0, tiled=True)

    def feed_in_out(got):
        got = got.reshape(n, LAYERS, rows, 2, unit_pad)[..., :units].astype(f32)
        return got.transpose(1, 2, 3, 0, 4).reshape(LAYERS, rows, 2 * FF)

    def body(
        hidden_in,
        positions,
        cotangent,
        attn_gain,
        qkv_weight,
        qkv_bias,
        out_weight,
        mlp_gain,
        in_weight,
        down_weight,
    ):
        me, me_z = lax.axis_index("ctx"), lax.axis_index("wt")
        shard = me * m + me_z
        offsets = ring.offsets(me)
        own_positions = positions[0]
        tokens = own_positions.shape[0]

        def spread(vector, width):
            row = jnp.zeros((1, QKV_W), bf16)
            return lax.dynamic_update_slice(row, vector[None], (0, shard * width))

        def qkv_block(l):
            rest = jnp.zeros((pad_rows - rows - 3, QKV_W), bf16)
            return jnp.concatenate(
                [
                    qkv_weight[l],
                    spread(qkv_bias[l], bias_w),
                    spread(attn_gain[l], rows),
                    spread(mlp_gain[l], rows),
                    rest,
                ]
            )

        def out_block(l):
            return jnp.pad(out_weight[l], ((0, pad_rows - rows), (0, 0)))

        def z_blocks(block):
            return ring.gather_z(block).reshape(step, block.shape[-1])

        def both_block(l):
            return jnp.concatenate([qkv_block(l), out_block(l)], axis=1)

        def z_parts(block):
            return [block] + [ring.swap_z(block, k) for k in range(1, m)]

        def z_join(parts):
            return jnp.concatenate(parts, axis=0)

        targets, sources = me ^ offsets, ring.sources(me)
        parts0 = z_parts(both_block(0))
        down0 = lax.all_gather(held(down_weight[0], *parts0), "wt", axis=0, tiled=True)
        cut = cut_columns(targets, [in_weight[l] for l in range(LAYERS)], units, unit_pad)
        steps0 = ring.gather_steps(held(z_join(parts0), cut[0]))
        own0 = next(steps0)
        traded = ring.trade([held(c, own0) for c in cut])
        pair0 = steps0.send(own0)
        traded[-1] = held(traded[-1], pair0)
        in0_got, in1_got = join_rows(sources, traded)
        in0 = lax.all_gather(held(in0_got, down0), "wt", axis=0, tiled=True)
        both0 = steps0.send(steps0.send(pair0))

        own_row = jnp.tile(own_positions, GROUP)[None]

        half_head = HEAD // 2
        frequency = jnp.exp(
            jnp.arange(half_head, dtype=f32) * (-2.0 * math.log(ROPE_BASE) / HEAD)
        )
        angles = own_positions.astype(f32)[:, None] * frequency[None, :]
        cos = jnp.tile(jnp.cos(angles), (1, 4))
        sin = jnp.tile(jnp.sin(angles), (1, 4))

        column = jnp.arange(all_rows, dtype=jnp.int32)
        in_block = column % pad_rows
        block_owner = ((me ^ offsets[:, None]) * m + (me_z ^ jnp.arange(m))[None, :]).reshape(-1)
        owner = jnp.repeat(block_owner, pad_rows)
        feature = jnp.where(in_block < rows, owner * rows + in_block, -1)
        every = jnp.arange(D, dtype=jnp.int32)
        perm = (every[:, None] == feature[None, :]).astype(bf16)
        second, first, inside = every // (n * rows), (every // rows) % n, every % rows
        perm2 = (every[:, None] == ((first * m + second) * rows + inside)[None, :]).astype(bf16)

        lane = jnp.arange(128, dtype=jnp.int32)[None]
        places = jnp.where(
            lane == 0, own_positions[:, None] // 256, jnp.where(lane == 1, own_positions[:, None] % 256, 0)
        ).astype(bf16)

        hidden0, rel0, query0, kv0, gain0 = before_attention(
            cfg, hidden_in[0], [], perm, cos, sin, both0, places
        )
        kvs0 = ring.gather(kv0)
        middle0, normed0, heads0, mix0, lse0, turn0 = attention(
            cfg, query0, kvs0, own_row, kvs0, hidden0, gain0, perm, perm2, both0, QKV_W
        )
        xs0 = ring.gather(normed0)
        steps1 = ring.gather_steps(z_join(z_parts(held(both_block(1), normed0))))
        own1 = next(steps1)
        xs0[-1] = held(xs0[-1], own1)
        keep, send, x_all0, units0, act0 = feed_forward(xs0, in0, down0)
        pair1 = held(steps1.send(own1), keep)
        in1 = lax.all_gather(held(in1_got, in0, xs0[1]), "wt", axis=0, tiled=True)
        total = ring.first(keep, send)
        while total.shape[0] > 2:
            total = ring.step(total)
        out = ring.outgoing(total)
        sums = (total[0], ring.move(total, out)[0])
        both1 = steps1.send(held(steps1.send(pair1), out))
        hidden1, rel1, query1, kv1, gain1 = before_attention(
            cfg, middle0, list(sums), perm, cos, sin, both1
        )
        kvs1 = ring.gather(kv1)
        down1_own = held(down_weight[1], in1, *kvs1)
        cotangent_late = held(cotangent[0], *kvs1)
        down1 = lax.all_gather(down1_own, "wt", axis=0, tiled=True)
        middle1, normed1, heads1, mix1, lse1, turn1 = attention(
            cfg, held(query1, down1_own, cotangent_late), kvs1, own_row, kvs0, hidden1, gain1, perm, perm2, both1, QKV_W
        )
        grads1 = ring.gather(cotangent_late, normed1)
        xs1 = ring.gather(normed1)

        def feed_reduce(keep, send, x_all, ugrad, act, g_all, *sc_behind):
            total = ring.first(keep, send)
            out = ring.outgoing(total)
            got = ring.move(total, out)
            in_terms = dot_rows(held(x_all, out), ugrad).astype(bf16)
            in_part = lax.psum_scatter(
                held(in_terms, *sc_behind), "wt", scatter_dimension=0, tiled=True
            )
            total = ring.add(total, got)
            while total.shape[0] > 2:
                total = ring.step(total)
            out = held(ring.outgoing(total), in_terms)
            got = ring.move(total, out)[0]
            down_terms = dot_rows(held(act, out), g_all)[:units].astype(bf16)
            return (total[0], held(got, down_terms)), in_part, down_terms

        keep, send, g_all1, ugrad1, x_all1, act1 = feed_forward_back(xs1, None, grads1, in1, down1)
        sums, in_part1, down_terms1 = feed_reduce(keep, send, x_all1, ugrad1, act1, g_all1)
        down_part1 = lax.psum_scatter(down_terms1, "wt", scatter_dimension=0, tiled=True)
        mgrad1, low1, mlp_gain_grad1, heads_grad1 = middle_back(
            cfg, sums, middle1, cotangent[0], gain1, perm, perm2, both1, QKV_W
        )
        keep, send, part1 = attention_back(
            cfg, heads_grad1, mix1, lse1, turn1, query1, kvs1, own_row, kvs0, cos, sin
        )
        kv_total = ring.first(keep, send)
        kv_out = ring.outgoing(kv_total)
        kv_got = ring.move(kv_total, kv_out)
        query_rel1 = query_back(cfg, held(part1, kv_out), both1)
        kv_sums = ring.finish(ring.add(kv_total, held(kv_got, query_rel1)))
        grad1, grad1_low, kv_part1, attn_gain_grad1 = layer_back(
            cfg, kv_sums, query_rel1, hidden1, mgrad1, gain1, cos, sin, perm, both1
        )
        grads0 = ring.gather(grad1_low)

        def wide_row(row):
            return jnp.pad(row[:1], ((0, 0), (0, QKV_W - D)))

        out_keep1, out_send1 = row_terms(heads1, held(low1, grad1_low))
        joint_keep1, joint_send1 = row_terms(
            rel1,
            jnp.concatenate([part1, kv_part1], axis=1),
            wide_row(attn_gain_grad1),
            wide_row(mlp_gain_grad1),
        )
        total1 = jnp.concatenate(
            [ring.first(out_keep1, out_send1), ring.first(joint_keep1, joint_send1)], axis=2
        )
        out1 = ring.outgoing(total1)
        cut = n // 2 * tokens
        act_late = held(act1, joint_send1)[:, :units]
        last_keep = dot(act_late[:cut], down1).astype(bf16)
        last_send = dot(act_late[cut:], down1).astype(bf16)
        hidden_total = ring.first(last_keep, last_send)
        hidden_out1 = ring.outgoing(hidden_total)
        grads0[-1] = held(grads0[-1], out1, hidden_out1)
        keep, send, g_all0, ugrad0 = feed_forward_back(None, units0, grads0, in0, down0)
        got1 = ring.move(total1, out1)
        hidden_got = ring.move(hidden_total, hidden_out1)
        sums, in_part0, down_terms0 = feed_reduce(
            keep, held(send, got1, hidden_got), x_all0, ugrad0, act0, g_all0, down_part1
        )
        mgrad0, low0, mlp_gain_grad0, heads_grad0 = middle_back(
            cfg, sums, middle0, grad1, gain0, perm, perm2, both0, QKV_W
        )
        total1 = ring.add(total1, held(got1, heads_grad0))
        while total1.shape[0] > 2:
            total1 = ring.step(total1)
        out1 = ring.outgoing(total1)
        hidden_total = ring.add(hidden_total, held(hidden_got, heads_grad0))
        while hidden_total.shape[0] > 2:
            hidden_total = ring.step(hidden_total)
        hidden_out1 = ring.outgoing(hidden_total)
        keep, send, part0 = attention_back(
            cfg, held(heads_grad0, out1, hidden_out1), mix0, lse0, turn0, query0, kvs0,
            own_row, kvs0, cos, sin,
        )
        got1 = ring.move(total1, out1)[0]
        hidden_got = ring.move(hidden_total, hidden_out1)[0]
        send = held(send, got1, hidden_got)
        kv_total = ring.first(keep, send)
        kv_out = ring.outgoing(kv_total)
        kv_got = ring.move(kv_total, kv_out)
        query_rel0 = query_back(cfg, held(part0, kv_out), both0)
        out_keep0, out_send0 = row_terms(heads0, held(low0, kv_out), mlp_gain_grad0[:1])
        kv_total = ring.add(kv_total, held(kv_got, query_rel0, out_send0))
        while kv_total.shape[0] > 2:
            kv_total = ring.step(kv_total)
        kv_out = ring.outgoing(kv_total)
        kv_got = ring.move(kv_total, kv_out)[0]
        query_keep0, query_send0 = row_terms(rel0, held(part0, kv_out))
        kv_sums = (kv_total[0], held(kv_got, query_send0))
        first0 = jnp.concatenate(
            [
                ring.first(out_keep0, out_send0),
                held(ring.first(query_keep0, query_send0), *kv_sums),
            ],
            axis=2,
        )
        first_out0 = ring.outgoing(first0)
        first_got0 = ring.move(first0, first_out0)
        down_in0 = held(down_terms0, in_part0)
        z_out1 = (total1[0] + held(got1, kv_got).astype(f32)).astype(bf16)
        z_out1 = z_out1.reshape(m, pad_rows, z_out1.shape[-1])
        z_got1 = [ring.swap_z(z_out1[k], k) for k in range(1, m)]
        grad0, unused, kv_part0, attn_gain_grad0 = layer_back(
            cfg, (kv_sums[0], held(kv_sums[1], first_out0, down_in0, z_out1)), query_rel0, hidden0, mgrad0, gain0, cos, sin, perm, both0
        )
        down_part0 = lax.psum_scatter(down_in0, "wt", scatter_dimension=0, tiled=True)
        hidden_out = middle1 + hidden_total[0] + held(hidden_got, grad0).astype(f32)
        first0 = ring.add(first0, first_got0)
        gain_rows = jnp.pad(attn_gain_grad0[:1], ((0, 127), (0, 0))).astype(bf16)
        columns = lax.dot_general(
            perm, gain_rows, (((0,), (1,)), ((), ())), preferred_element_type=f32
        ).astype(bf16)
        cut = all_rows // 2
        kv_keep0, kv_send0 = [
            jnp.concatenate([half, columns[i * cut : (i + 1) * cut]], axis=1)
            for i, half in enumerate(row_terms(rel0, kv_part0))
        ]
        last0 = ring.first(kv_keep0, kv_send0)
        last_out0 = ring.outgoing(last0)
        last_got0 = ring.move(last0, last_out0)
        home = feed_in_home([held(in_part0, last_got0), in_part1])
        last0 = ring.add(last0, last_got0)
        total0 = jnp.concatenate([first0, last0], axis=2)
        while total0.shape[0] > 2:
            total0 = ring.step(total0)
        last_got0 = ring.move(total0, ring.outgoing(total0))[0]
        last_sum0 = (total0[0] + held(last_got0, down_part0).astype(f32)).astype(bf16)
        layer0 = ring.reduce_z(last_sum0.reshape(m, pad_rows, last_sum0.shape[-1]))
        layer1 = sum((held(g, layer0).astype(f32) for g in z_got1), z_out1[0].astype(f32))
        gain_at = QW + QKV_W

        def own_part(row, width):
            return lax.dynamic_slice(row, (0, shard * width), (1, width))[0]

        stacked = [
            jnp.stack([layer0[:rows, gain_at], own_part(layer1[rows + 1 : rows + 2, QW:], rows)]),
            jnp.stack([layer[:rows, QW : QW + QKV_W] for layer in (layer0, layer1)]),
            jnp.stack(
                [own_part(l[rows : rows + 1, QW : QW + QKV_W], bias_w) for l in (layer0, layer1)]
            ),
            jnp.stack([layer[:rows, :QW] for layer in (layer0, layer1)]),
            jnp.stack(
                [
                    own_part(layer0[rows + 1 : rows + 2, :QW], rows),
                    own_part(layer1[rows + 2 : rows + 3, QW:], rows),
                ]
            ),
        ]
        in_weight_grad = feed_in_out(held(home, last_sum0))
        down_weight_grad = jnp.stack([down_part0, down_part1]).astype(f32)
        return (hidden_out[None], grad0[None], *stacked, in_weight_grad, down_weight_grad)

    return body


def solution(mesh):
    sizes = dict(mesh.shape)
    rows = P("wt", "ctx", None)
    vector = P(None, ("ctx", "wt"))
    matrix = P(None, ("ctx", "wt"), None)
    return jax.shard_map(
        make_body(sizes["ctx"], sizes["wt"]),
        mesh=mesh,
        in_specs=(
            rows, P("wt", "ctx"), rows, vector, matrix, vector, matrix, vector, matrix, matrix,
        ),
        out_specs=(rows, rows, vector, matrix, vector, matrix, vector, matrix, matrix),
        check_vma=False,
    )
```

```python
import functools
import math

import jax
import jax.numpy as jnp
from jax import lax
from jax.experimental import pallas as pl
from jax.experimental.pallas import tpu as pltpu
from jax.sharding import PartitionSpec as P

HEADS = 14
KV_HEADS = 2
GROUP = HEADS // KV_HEADS
HEAD = 64
FF = 4864
LAYERS = 2
QW = 896
D = 896
QKV_W = 1152
KV_W = KV_HEADS * HEAD

EPSILON = 1e-06
ROPE_BASE = 1000000.0
NEGATIVE = -1e30
SCALE = HEAD**-0.5

bf16 = jnp.bfloat16
f32 = jnp.float32

ANY = pl.BlockSpec(memory_space=pl.ANY)
VMEM = pl.BlockSpec(memory_space=pltpu.VMEM)
DMA = pltpu.SemaphoreType.DMA


def shape(dims, dtype):
    return jax.ShapeDtypeStruct(dims, dtype)


def dot(left, right):
    return jnp.dot(left, right, preferred_element_type=f32)


def dot_rows(left, right):
    return lax.dot_general(left, right, (((0,), (0,)), ((), ())), preferred_element_type=f32)


def dot_cols(left, right):
    return lax.dot_general(left, right, (((1,), (1,)), ((), ())), preferred_element_type=f32)


class Lazy:
    def __init__(self, ref, copy):
        self.ref, self.copy = ref, copy

    def __getitem__(self, at):
        if self.copy is not None:
            self.copy.wait()
            self.copy = None
        return self.ref[at]


class Late:
    def __init__(self, ref, target, sem):
        self.ref, self.copy = ref, pltpu.make_async_copy(ref, target, sem)
        self.sent = False

    def __getitem__(self, at):
        return self.ref[at]

    def __setitem__(self, at, value):
        self.ref[at] = value

    def flush(self):
        self.copy.start()
        self.sent = True


def lazily(kernel, ins, in_specs, outs, out_specs, scratch):
    n_in, n_out = len(ins), len(outs)
    staged = [i for i, spec in enumerate(in_specs) if spec is VMEM]
    late = [i for i, spec in enumerate(out_specs) if spec is VMEM]
    n_scratch = len(scratch)

    def whole(*refs):
        refs = list(refs)
        own = refs[n_in + n_out + n_scratch :]
        ins_v, outs_v = own[: len(staged)], own[len(staged) : len(staged) + len(late)]
        in_sems, out_sems = own[-2:]
        for k, i in enumerate(staged):
            copy = pltpu.make_async_copy(refs[i], ins_v[k], in_sems.at[k])
            copy.start()
            refs[i] = Lazy(ins_v[k], copy)
        results = []
        for k, i in enumerate(late):
            results.append(Late(outs_v[k], refs[n_in + i], out_sems.at[k]))
            refs[n_in + i] = results[-1]
        kernel(*refs[: n_in + n_out + n_scratch])
        for i in staged:
            if refs[i].copy is not None:
                refs[i].copy.wait()
        for result in results:
            if not result.sent:
                result.flush()
        for result in results:
            result.copy.wait()

    scratch = [
        *scratch,
        *[pltpu.VMEM(ins[i].shape, ins[i].dtype) for i in staged],
        *[pltpu.VMEM(outs[i].shape, outs[i].dtype) for i in late],
        DMA((max(len(staged), 1),)),
        DMA((max(len(late), 1),)),
    ]
    in_specs = [ANY if spec is VMEM else spec for spec in in_specs]
    out_specs = [ANY if spec is VMEM else spec for spec in out_specs]
    return whole, in_specs, out_specs, scratch


def run(kernel, ins, in_specs, outs, out_specs, scratch, flops, vmem=60, lazy=False):
    if lazy:
        kernel, in_specs, out_specs, scratch = lazily(
            kernel, ins, in_specs, outs, out_specs, scratch
        )
    moved = sum(math.prod(x.shape) * x.dtype.itemsize for x in [*ins, *outs])
    return pl.pallas_call(
        kernel,
        out_shape=outs,
        in_specs=in_specs,
        out_specs=out_specs,
        scratch_shapes=scratch,
        compiler_params=pltpu.CompilerParams(vmem_limit_bytes=vmem * 2**20),
        cost_estimate=pl.CostEstimate(flops=flops, bytes_accessed=moved, transcendentals=0),
    )(*ins)


def copies(sources, targets, sems):
    made = [pltpu.make_async_copy(s, t, sems.at[i]) for i, (s, t) in enumerate(zip(sources, targets))]
    for c in made:
        c.start()
    return made


def rows_of(ref, count, size):
    return [ref.at[pl.ds(i * size, size)] for i in range(count)]


class Blocks:
    def __init__(self, arrays, places):
        self.arrays, self.places = arrays, places

    def take(self, it):
        refs = [next(it) for _ in self.arrays]
        return [refs[a].at[b] for a, b in self.places]


def turned(block):
    lane = lax.broadcasted_iota(jnp.int32, block.shape, 1)
    return jnp.where(lane % HEAD < HEAD // 2, -pltpu.roll(block, 96, 1), pltpu.roll(block, 32, 1))


def rotated(block, cos, sin):
    return block * cos + turned(block) * sin


def rotated_back(block, cos, sin):
    return block * cos - turned(block) * sin


def inverse_norm(hidden):
    return lax.rsqrt(jnp.mean(hidden * hidden, axis=-1, keepdims=True) + EPSILON)


def norm_back(normed_grad, hidden, gain):
    inverse = inverse_norm(hidden)
    scaled = normed_grad * gain
    inner = jnp.mean(scaled * hidden, axis=-1, keepdims=True)
    into = inverse * scaled - hidden * (inverse * inverse * inverse * inner)
    return into, jnp.sum(normed_grad * (hidden * inverse), axis=0, keepdims=True)


def split_dot_cols(value, right):
    high = value.astype(bf16)
    low = (value - high.astype(f32)).astype(bf16)
    return dot_cols(high, right) + dot_cols(low, right)


def first_row(row):
    return jnp.broadcast_to(row, (8, row.shape[1]))


def before_attention(cfg, base, sums, perm, cos, sin, blocks, places=None):
    n, m, rows, pad_rows = cfg
    tokens, step = base.shape[0], m * pad_rows
    all_rows = n * step
    more = [] if places is None else [places]

    def kernel(*refs):
        it = iter(refs)
        more_refs = [next(it) for _ in more]
        base_ref = next(it)
        sum_refs = [next(it) for _ in sums]
        perm_ref, cos_ref, sin_ref = next(it), next(it), next(it)
        block_refs = blocks.take(it)
        hidden_ref, rel_ref, query_ref, kv_ref, gain_ref, weight, sems = it
        waits = copies(
            [b.at[:, pl.ds(0, QKV_W)] for b in block_refs], rows_of(weight, n, step), sems
        )
        hidden = base_ref[...].astype(f32)
        for ref in sum_refs:
            hidden = hidden + ref[...].astype(f32)
        hidden_ref[...] = hidden
        scaled = hidden * inverse_norm(hidden)
        cos, sin = cos_ref[...], sin_ref[...]
        for w in waits:
            w.wait()
        last = jnp.zeros((16, QKV_W), f32)
        for i in range(n * m):
            last = last + weight[pl.ds((i + 1) * pad_rows - 16, 16), :].astype(f32)
        at = rows + 1 - (pad_rows - 16)
        gain_ref[0:8, :] = first_row(last[at : at + 1, :D])
        gain_ref[8:16, :] = first_row(last[at + 1 : at + 2, :D])
        normed = (scaled * last[at : at + 1, :D]).astype(bf16)
        rel = dot(normed, perm_ref[...])
        lane = lax.broadcasted_iota(jnp.int32, rel.shape, 1)
        rel = jnp.where(lane % pad_rows == rows, 1.0, rel).astype(bf16)
        rel_ref[...] = rel
        kv = dot(rel, weight[:, QW:])
        kv_ref[:, :KV_W] = rotated(kv[:, :KV_W], cos, sin).astype(bf16)
        kv_ref[:, KV_W : 2 * KV_W] = kv[:, KV_W:].astype(bf16)
        for ref in more_refs:
            kv_ref[:, 2 * KV_W :] = ref[...]
        query = dot(rel, weight[:, :QW])
        for i in range(QW // 128):
            part = rotated(query[:, i * 128 : (i + 1) * 128], cos, sin).astype(bf16)
            query_ref[:, i * 128 : (i + 1) * 128] = part * SCALE

    ins = [*more, base, *sums, perm, cos, sin]
    return run(
        kernel,
        [*ins, *blocks.arrays],
        [VMEM] * len(ins) + [ANY] * len(blocks.arrays),
        [
            shape((tokens, D), f32),
            shape((tokens, all_rows), bf16),
            shape((tokens, QW), bf16),
            shape((tokens, 2 * KV_W + 128 * len(more)), bf16),
            shape((16, D), f32),
        ],
        [VMEM] * 5,
        [pltpu.VMEM((all_rows, QKV_W), bf16), DMA((n,))],
        2 * tokens * all_rows * (D + QKV_W),
    )


def kv_copies(n, tokens, kv_refs, place_refs, kv, place, sems):
    return copies(
        [
            *[r.at[:, pl.ds(0, 2 * KV_W)] for r in kv_refs],
            *[r.at[:, pl.ds(2 * KV_W, 128)] for r in place_refs],
        ],
        [*rows_of(kv, n, tokens), *rows_of(place, n, tokens)],
        sems,
    )


def place_column(place, at):
    block = place[at, :].astype(f32)
    return (block[:, 0:1] * 256.0 + block[:, 1:2]).astype(jnp.int32)


def heads_to_lanes(matrix, group, tokens):
    parts = [
        matrix[(group * GROUP + h) * HEAD : (group * GROUP + h + 1) * HEAD, :] for h in range(GROUP)
    ]
    return jnp.concatenate(parts, axis=1)


def lanes_to_heads(groups, tokens):
    parts = [g[:, h * tokens : (h + 1) * tokens] for g in groups for h in range(GROUP)]
    return jnp.concatenate(parts, axis=0).T


def heads_to_rows(matrix, group):
    parts = [
        matrix[:, (group * GROUP + h) * HEAD : (group * GROUP + h + 1) * HEAD] for h in range(GROUP)
    ]
    return jnp.concatenate(parts, axis=0)


def attention(
    cfg, query, kv_blocks, own_row, place_blocks, hidden, gain, perm, perm2, out_blocks, out_at
):
    n, m, rows, pad_rows = cfg
    tokens, step = query.shape[0], m * pad_rows
    all_rows, wide = n * step, GROUP * query.shape[0]
    slots = KV_HEADS if n <= 8 else 1

    def kernel(*refs):
        it = iter(refs)
        query_ref = next(it)
        kv_refs = [next(it) for _ in range(n)]
        place_refs = [next(it) for _ in range(n)]
        row_ref, hidden_ref, gain_ref, perm_in, perm2_in = [next(it) for _ in range(5)]
        out_refs = out_blocks.take(it)
        middle_ref, normed_ref, rel_ref, mix_ref, lse_ref, turn_ref = [next(it) for _ in range(6)]
        kv, place, values_t, scores = [next(it) for _ in range(4)]
        probs = next(it) if slots > 1 else None
        perm_v, perm2_v, weight, kv_sems, sems = it
        kv_waits = kv_copies(n, tokens, kv_refs, place_refs, kv, place, kv_sems)
        waits = copies(
            [perm_in, perm2_in, *[o.at[:, pl.ds(out_at, D)] for o in out_refs]],
            [perm_v, perm2_v, *rows_of(weight, n, step)],
            sems,
        )
        query_t = query_ref[...].astype(f32).T
        for w in kv_waits:
            w.wait()
        for g in range(KV_HEADS):
            turn_ref[g * HEAD : (g + 1) * HEAD, :] = heads_to_lanes(query_t, g, tokens).astype(bf16)

        if probs is None:
            for j in range(n):
                block = kv[pl.ds(j * tokens, tokens), KV_W:]
                values_t[j] = block.astype(f32).T.astype(bf16)
        else:
            values_t[...] = kv[:, KV_W:].astype(f32).T.astype(bf16)
        own = row_ref[...]
        mixed = []
        for g in range(KV_HEADS):
            turn = turn_ref[g * HEAD : (g + 1) * HEAD, :]
            top = jnp.full((1, wide), NEGATIVE, f32)
            for j in range(n):
                at = pl.ds(j * tokens, tokens)
                s = dot(kv[at, g * HEAD : (g + 1) * HEAD], turn)
                s = jnp.where(place_column(place, at) <= own, s, NEGATIVE)
                scores[g % slots, at, :] = s
                top = jnp.maximum(top, jnp.max(s, axis=0, keepdims=True))
            total = jnp.zeros((1, wide), f32)
            out = jnp.zeros((HEAD, wide), f32)
            for j in range(n):
                at = pl.ds(j * tokens, tokens)
                p = jnp.exp(scores[g % slots, at, :] - top)
                total = total + jnp.sum(p, axis=0, keepdims=True)
                if probs is None:
                    out = out + dot(values_t[j, g * HEAD : (g + 1) * HEAD, :], p.astype(bf16))
                else:
                    probs[g, at, :] = p.astype(bf16)
            if probs is not None:
                out = dot(values_t[g * HEAD : (g + 1) * HEAD, :], probs[g])
            out = out / total
            mix_ref[g * HEAD : (g + 1) * HEAD, :] = out
            lse_ref[g * 8 : (g + 1) * 8, :] = first_row(top + jnp.log(total))
            mixed.append(out)
        heads = lanes_to_heads(mixed, tokens).astype(bf16)
        for w in waits:
            w.wait()
        rel = dot(heads, perm_v[...]).astype(bf16)
        rel_ref[...] = rel
        middle = hidden_ref[...] + dot(rel, weight[...])
        middle_ref[...] = middle
        normed = (middle * inverse_norm(middle) * gain_ref[8:9, :]).astype(bf16)
        normed_ref[...] = dot(normed, perm2_v[...]).astype(bf16)

    return run(
        kernel,
        [query, *kv_blocks, *place_blocks, own_row, hidden, gain, perm, perm2, *out_blocks.arrays],
        [VMEM] + [ANY] * (2 * n) + [VMEM] * 3 + [ANY] * (len(out_blocks.arrays) + 2),
        [
            shape((tokens, D), f32),
            shape((tokens, D), bf16),
            shape((tokens, all_rows), bf16),
            shape((KV_W, wide), f32),
            shape((16, wide), f32),
            shape((KV_W, wide), bf16),
        ],
        [VMEM] * 6,
        [
            pltpu.VMEM((n * tokens, 2 * KV_W), bf16),
            pltpu.VMEM((n * tokens, 128), bf16),
            pltpu.VMEM((KV_W, n * tokens) if slots > 1 else (n, KV_W, tokens), bf16),
            pltpu.VMEM((slots, n * tokens, wide), f32),
            *([pltpu.VMEM((slots, n * tokens, wide), bf16)] if slots > 1 else []),
            pltpu.VMEM((D, all_rows), bf16),
            pltpu.VMEM((D, D), bf16),
            pltpu.VMEM((all_rows, D), bf16),
            DMA((2 * n,)),
            DMA((n + 2,)),
        ],
        8 * tokens * n * tokens * QW,
        60,
    )


def middle_back(cfg, sums, middle, gradient, gain, perm, perm2, out_blocks, out_at):
    n, m, rows, pad_rows = cfg
    tokens, step = middle.shape[0], m * pad_rows
    all_rows = n * step

    def kernel(*refs):
        it = iter(refs)
        sum_refs = [next(it), next(it)]
        middle_ref, grad_ref, gain_ref, perm_in, perm2_ref = [next(it) for _ in range(5)]
        out_refs = out_blocks.take(it)
        mgrad_ref, low_ref, gain_grad_ref, heads_ref = [next(it) for _ in range(4)]
        perm_v, weight, sems = it
        waits = copies(
            [perm_in, *[o.at[:, pl.ds(out_at, D)] for o in out_refs]],
            [perm_v, *rows_of(weight, n, step)],
            sems,
        )
        normed_grad = split_dot_cols(
            sum_refs[0][...] + sum_refs[1][...].astype(f32), perm2_ref[...]
        )
        into, gain_grad = norm_back(normed_grad, middle_ref[...], gain_ref[8:9, :])
        middle_grad = grad_ref[...].astype(f32) + into
        mgrad_ref[...] = middle_grad
        gain_grad_ref[...] = first_row(gain_grad)
        low = middle_grad.astype(bf16)
        low_ref[...] = low
        for w in waits:
            w.wait()
        heads_rel = dot_cols(low, weight[...]).astype(bf16)
        heads_ref[...] = dot_cols(heads_rel, perm_v[...]).astype(bf16)

    return run(
        kernel,
        [*sums, middle, gradient, gain, perm, perm2, *out_blocks.arrays],
        [VMEM] * 5 + [ANY] + [VMEM] + [ANY] * len(out_blocks.arrays),
        [
            shape((tokens, D), f32),
            shape((tokens, D), bf16),
            shape((8, D), f32),
            shape((tokens, QW), bf16),
        ],
        [VMEM] * 4,
        [pltpu.VMEM((D, all_rows), bf16), pltpu.VMEM((all_rows, D), bf16), DMA((n + 1,))],
        2 * tokens * D * (2 * D + 2 * all_rows),
    )


def attention_back(
    cfg, heads_grad, mix, lse, turn, query, kv_blocks, own_row, place_blocks, cos, sin
):
    n, m, rows, pad_rows = cfg
    tokens, half = query.shape[0], n // 2
    wide = GROUP * query.shape[0]

    def kernel(*refs):
        it = iter(refs)
        heads_ref, mix_ref, lse_ref, turn_ref, query_ref = [next(it) for _ in range(5)]
        kv_refs = [next(it) for _ in range(n)]
        place_refs = [next(it) for _ in range(n)]
        row_ref, cos_ref, sin_ref = [next(it) for _ in range(3)]
        keep_ref, send_ref, part_ref = [next(it) for _ in range(3)]
        kv, place, keys_t, probs, score_grads, kv_sems = it
        kv_waits = kv_copies(n, tokens, kv_refs, place_refs, kv, place, kv_sems)
        heads = heads_ref[...]
        heads_t = heads.astype(f32).T
        for w in kv_waits:
            w.wait()
        keys_t[...] = kv[:, :KV_W].astype(f32).T.astype(bf16)
        own = row_ref[...]
        query = query_ref[...]
        sides = []
        for g in range(KV_HEADS):
            grad_t = heads_to_lanes(heads_t, g, tokens)
            inner = jnp.sum(mix_ref[g * HEAD : (g + 1) * HEAD, :] * grad_t, axis=0, keepdims=True)
            sides.append(
                (
                    turn_ref[g * HEAD : (g + 1) * HEAD, :],
                    heads_to_rows(query, g),
                    grad_t.astype(bf16),
                    heads_to_rows(heads, g),
                    inner,
                    lse_ref[g * 8 : g * 8 + 1, :],
                )
            )
        wholes = []
        for g, (turn, query_rows, grad_t, grad_rows, inner, lse) in enumerate(sides):
            for j in range(n):
                at = pl.ds(j * tokens, tokens)
                s = dot(kv[at, g * HEAD : (g + 1) * HEAD], turn)
                p = jnp.exp(jnp.where(place_column(place, at) <= own, s, NEGATIVE) - lse)
                prob_grad = dot(kv[at, KV_W + g * HEAD : KV_W + (g + 1) * HEAD], grad_t)
                probs[at, :] = p.astype(bf16)
                score_grads[at, :] = (p * (prob_grad - inner)).astype(bf16)
            for part, ref in enumerate([keep_ref, send_ref]):
                at = pl.ds(part * half * tokens, half * tokens)
                key_out = dot(score_grads[at, :], query_rows).astype(bf16)
                value_out = dot(probs[at, :], grad_rows).astype(bf16)
                ref[:, g * HEAD : (g + 1) * HEAD] = key_out
                ref[:, KV_W + g * HEAD : KV_W + (g + 1) * HEAD] = value_out
            wholes.append(dot(keys_t[g * HEAD : (g + 1) * HEAD, :], score_grads[...]))
        keep_ref.flush()
        send_ref.flush()
        whole = lanes_to_heads(wholes, tokens) * SCALE
        cos, sin = cos_ref[...], sin_ref[...]
        for i in range(QW // 128):
            at = slice(i * 128, (i + 1) * 128)
            part_ref[:, at] = rotated_back(whole[:, at], cos, sin).astype(bf16)

    return run(
        kernel,
        [heads_grad, mix, lse, turn, query, *kv_blocks, *place_blocks, own_row, cos, sin],
        [VMEM] * 5 + [ANY] * (2 * n) + [VMEM] * 3,
        [
            shape((half * tokens, 2 * KV_W), bf16),
            shape((half * tokens, 2 * KV_W), bf16),
            shape((tokens, QW), bf16),
        ],
        [VMEM] * 3,
        [
            pltpu.VMEM((n * tokens, 2 * KV_W), bf16),
            pltpu.VMEM((n * tokens, 128), bf16),
            pltpu.VMEM((KV_W, n * tokens), bf16),
            pltpu.VMEM((n * tokens, wide), bf16),
            pltpu.VMEM((n * tokens, wide), bf16),
            DMA((2 * n,)),
        ],
        20 * tokens * n * tokens * QW,
        60,
        lazy=True,
    )


def query_back(cfg, query_part, blocks):
    n, m, rows, pad_rows = cfg
    tokens, step = query_part.shape[0], m * pad_rows

    def kernel(*refs):
        it = iter(refs)
        part_ref, block_refs = next(it), blocks.take(it)
        out_ref, weight, sems = it
        waits = copies(
            [b.at[:, pl.ds(0, QW)] for b in block_refs], rows_of(weight, n, step), sems
        )
        for w in waits:
            w.wait()
        out_ref[...] = dot_cols(part_ref[...], weight[...])

    return run(
        kernel,
        [query_part, *blocks.arrays],
        [VMEM] + [ANY] * len(blocks.arrays),
        [shape((tokens, n * step), f32)],
        [VMEM],
        [pltpu.VMEM((n * step, QW), bf16), DMA((n,))],
        2 * tokens * n * step * QW,
        lazy=True,
    )[0]


def layer_back(cfg, sums, query_rel, hidden, middle_grad, gain, cos, sin, perm, blocks):
    n, m, rows, pad_rows = cfg
    tokens, step = hidden.shape[0], m * pad_rows

    def kernel(*refs):
        it = iter(refs)
        sum_refs = [next(it), next(it)]
        rel_ref, hidden_ref, mgrad_ref, gain_ref, cos_ref, sin_ref, perm_ref = [
            next(it) for _ in range(7)
        ]
        block_refs = blocks.take(it)
        grad_ref, low_ref, part_ref, gain_grad_ref, weight, sems = it
        waits = copies(
            [b.at[:, pl.ds(QW, 2 * KV_W)] for b in block_refs], rows_of(weight, n, step), sems
        )
        total = sum_refs[0][...] + sum_refs[1][...].astype(f32)
        keys = rotated_back(total[:, :KV_W], cos_ref[...], sin_ref[...])
        part = jnp.concatenate([keys, total[:, KV_W:]], axis=1).astype(bf16)
        part_ref[...] = part
        part_ref.flush()
        for w in waits:
            w.wait()
        rel = rel_ref[...] + dot_cols(part, weight[...])
        normed_grad = split_dot_cols(rel, perm_ref[...])
        into, gain_grad = norm_back(normed_grad, hidden_ref[...], gain_ref[0:1, :])
        gradient = mgrad_ref[...] + into
        grad_ref[...] = gradient
        low_ref[...] = gradient.astype(bf16)
        gain_grad_ref[...] = first_row(gain_grad)

    return run(
        kernel,
        [*sums, query_rel, hidden, middle_grad, gain, cos, sin, perm, *blocks.arrays],
        [VMEM] * 9 + [ANY] * len(blocks.arrays),
        [
            shape((tokens, D), f32),
            shape((tokens, D), bf16),
            shape((tokens, 2 * KV_W), bf16),
            shape((8, D), f32),
        ],
        [VMEM] * 4,
        [pltpu.VMEM((n * step, 2 * KV_W), bf16), DMA((n,))],
        2 * tokens * n * step * (2 * KV_W + 2 * D),
        lazy=True,
    )


def gated(gate, up):
    return gate * jax.nn.sigmoid(gate) * up


def gated_back(act_grad, gate, up):
    sig = jax.nn.sigmoid(gate)
    gate_grad = act_grad * up * (sig * (1.0 + gate * (1.0 - sig)))
    return gate_grad, act_grad * (gate * sig)


def feed_forward(x_blocks, in_proj, down_proj):
    n, tokens, units, width = len(x_blocks), x_blocks[0].shape[0], down_proj.shape[0], in_proj.shape[1]
    half, pad, total = n // 2, width // 2, n * tokens

    def kernel(*refs):
        x_refs, (in_ref, down_ref) = refs[:n], refs[n : n + 2]
        keep_ref, send_ref, all_ref, unit_ref, act_ref = refs[n + 2 : n + 7]
        x, w_in, w_down, units_v, act_v, terms, x_sems, w_sems, o_sems = refs[n + 7 :]
        in_wait, down_wait = copies([in_ref, down_ref], [w_in, w_down.at[pl.ds(0, units)]], w_sems)
        x_waits = copies(x_refs, rows_of(x, n, tokens), x_sems)
        if pad > units:
            w_down[units:, :] = jnp.zeros((pad - units, D), bf16)
        in_wait.wait()
        down_wait.wait()
        outs = []

        def put(src, dst, slot):
            copy = pltpu.make_async_copy(src, dst, o_sems.at[slot])
            copy.start()
            outs.append(copy)

        big = half * tokens
        for i, (part, target) in enumerate([(1, send_ref), (0, keep_ref)]):
            at = pl.ds(part * big, big)
            for w in x_waits[part * half : (part + 1) * half]:
                w.wait()
            put(x.at[at], all_ref.at[at], 4 * i)
            both = dot(x[at, :], w_in[...])
            units_v[at, :] = both.astype(bf16)
            put(units_v.at[at], unit_ref.at[at], 4 * i + 1)
            act = gated(both[:, :pad], both[:, pad:]).astype(bf16)
            act_v[at, :] = act
            put(act_v.at[at], act_ref.at[at], 4 * i + 2)
            terms[part] = dot(act, w_down[...]).astype(bf16)
            put(terms.at[part], target, 4 * i + 3)
        for copy in outs:
            copy.wait()

    return run(
        kernel,
        [*x_blocks, in_proj, down_proj],
        [ANY] * (n + 2),
        [
            shape((half * tokens, D), bf16),
            shape((half * tokens, D), bf16),
            shape((total, D), bf16),
            shape((total, width), bf16),
            shape((total, pad), bf16),
        ],
        [ANY] * 5,
        [
            pltpu.VMEM((total, D), bf16),
            pltpu.VMEM((D, width), bf16),
            pltpu.VMEM((pad, D), bf16),
            pltpu.VMEM((total, width), bf16),
            pltpu.VMEM((total, pad), bf16),
            pltpu.VMEM((2, half * tokens, D), bf16),
            DMA((n,)),
            DMA((2,)),
            DMA((8,)),
        ],
        2 * total * D * (width + pad),
        60,
    )


def feed_forward_back(x_blocks, units_all, grad_blocks, in_proj, down_proj):
    n, tokens = len(grad_blocks), grad_blocks[0].shape[0]
    units, width = down_proj.shape[0], in_proj.shape[1]
    half, pad, total = n // 2, width // 2, n * tokens
    fresh = units_all is None

    def kernel(*refs):
        it = iter(refs)
        x_refs = [next(it) for _ in range(n)] if fresh else []
        unit_ref = None if fresh else next(it)
        g_refs = [next(it) for _ in range(n)]
        in_ref, down_ref = next(it), next(it)
        keep_ref, send_ref, gall_ref, ugrad_ref = [next(it) for _ in range(4)]
        all_ref, act_ref = (next(it), next(it)) if fresh else (None, None)
        g, w_in, w_down, ugrad, terms = [next(it) for _ in range(5)]
        x, act_v = (next(it), next(it)) if fresh else (None, None)
        units_v = None if fresh else next(it)
        g_sems, w_sems, o_sems, x_sems = it
        in_wait, down_wait = copies([in_ref, down_ref], [w_in, w_down.at[pl.ds(0, units)]], w_sems)
        g_waits = copies(g_refs, rows_of(g, n, tokens), g_sems)
        if fresh:
            x_waits = copies(x_refs, rows_of(x, n, tokens), x_sems)
        else:
            x_waits = copies(rows_of(unit_ref, n, tokens), rows_of(units_v, n, tokens), x_sems)
        if pad > units:
            w_down[units:, :] = jnp.zeros((pad - units, D), bf16)
        in_wait.wait()
        down_wait.wait()
        outs = []

        def put(src, dst, slot):
            copy = pltpu.make_async_copy(src, dst, o_sems.at[slot])
            copy.start()
            outs.append(copy)

        big = half * tokens
        for i, (part, target) in enumerate([(1, send_ref), (0, keep_ref)]):
            at = pl.ds(part * big, big)
            for w in x_waits[part * half : (part + 1) * half]:
                w.wait()
            if fresh:
                put(x.at[at], all_ref.at[at], 5 * i)
                both = dot(x[at, :], w_in[...])
                gate, up = both[:, :pad], both[:, pad:]
                act_v[at, :] = gated(gate, up).astype(bf16)
                put(act_v.at[at], act_ref.at[at], 5 * i + 1)
            else:
                gate, up = units_v[at, :pad].astype(f32), units_v[at, pad:].astype(f32)
            for w in g_waits[part * half : (part + 1) * half]:
                w.wait()
            put(g.at[at], gall_ref.at[at], 5 * i + 2)
            gate_grad, up_grad = gated_back(dot_cols(g[at, :], w_down[...]), gate, up)
            ugrad[at, :pad] = gate_grad.astype(bf16)
            ugrad[at, pad:] = up_grad.astype(bf16)
            put(ugrad.at[at], ugrad_ref.at[at], 5 * i + 3)
            terms[part] = dot_cols(ugrad[at, :], w_in[...]).astype(bf16)
            put(terms.at[part], target, 5 * i + 4)
        for copy in outs:
            copy.wait()

    ins = [*(x_blocks if fresh else [units_all]), *grad_blocks, in_proj, down_proj]
    outs = [
        shape((half * tokens, D), bf16),
        shape((half * tokens, D), bf16),
        shape((total, D), bf16),
        shape((total, width), bf16),
    ]
    scratch = [
        pltpu.VMEM((total, D), bf16),
        pltpu.VMEM((D, width), bf16),
        pltpu.VMEM((pad, D), bf16),
        pltpu.VMEM((total, width), bf16),
        pltpu.VMEM((2, half * tokens, D), bf16),
    ]
    if fresh:
        outs += [shape((total, D), bf16), shape((total, pad), bf16)]
        scratch += [pltpu.VMEM((total, D), bf16), pltpu.VMEM((total, pad), bf16)]
    else:
        scratch += [pltpu.VMEM((total, width), bf16)]
    scratch += [DMA((n,)), DMA((2,)), DMA((10,)), DMA((n,))]
    return run(
        kernel,
        ins,
        [ANY] * len(ins),
        outs,
        [ANY] * len(outs),
        scratch,
        2 * total * D * (width * (2 if fresh else 1) + pad),
        60,
    )


def cut_columns(order, weights, units, unit_pad):
    n, (rows, _), layers = order.shape[0], weights[0].shape, len(weights)

    def kernel(order_ref, *refs):
        weight_refs, outs, parts = refs[:layers], refs[layers:-1], refs[-1]
        zeros = jnp.zeros((rows, unit_pad - units), bf16)
        for l in range(layers):
            for c in range(n):
                for k in range(2):
                    at, to = k * FF + c * units, k * unit_pad
                    parts[c, l, :, to : to + units] = weight_refs[l][:, at : at + units]
                    if unit_pad > units:
                        parts[c, l, :, to + units : to + unit_pad] = zeros
        for a in range(n):
            outs[a][...] = parts[order_ref[a]]

    return run(
        kernel,
        [order, *weights],
        [pl.BlockSpec(memory_space=pltpu.SMEM)] + [VMEM] * layers,
        [shape((layers, rows, 2 * unit_pad), bf16)] * n,
        [VMEM] * n,
        [pltpu.VMEM((n, layers, rows, 2 * unit_pad), bf16)],
        0,
    )


def join_rows(order, blocks):
    n, (layers, rows, width) = len(blocks), blocks[0].shape

    def kernel(order_ref, *refs):
        block_refs, outs, parts = refs[:n], refs[n:-1], refs[-1]
        for a in range(n):
            parts[order_ref[a]] = block_refs[a][...]
        for l in range(layers):
            for c in range(n):
                outs[l][c * rows : (c + 1) * rows, :] = parts[c, l]

    return run(
        kernel,
        [order, *blocks],
        [pl.BlockSpec(memory_space=pltpu.SMEM)] + [VMEM] * n,
        [shape((n * rows, width), bf16)] * layers,
        [VMEM] * layers,
        [pltpu.VMEM((n, layers, rows, width), bf16)],
        0,
    )


class Ring:
    def __init__(self, n, m):
        self.n, self.m = n, m
        if n == 8:
            self.even = [0, 4, 2, 6, 1, 3, 5, 7]
            self.odd = [0, 2, 4, 6, 1, 5, 3, 7]
        else:
            self.even = self.odd = list(range(n))

    def swap(self, value, offset, odd_offset=None):
        odd_offset = offset if odd_offset is None else odd_offset
        return lax.ppermute(
            value, "ctx", [(i, i ^ (odd_offset if i % 2 else offset)) for i in range(self.n)]
        )

    def swap_z(self, value, offset):
        return lax.ppermute(value, "wt", [(i, i ^ offset) for i in range(self.m)])

    def offsets(self, me):
        return jnp.where(
            me % 2 == 1, jnp.array(self.odd, jnp.int32), jnp.array(self.even, jnp.int32)
        )

    def gather(self, own, *behind, places=(0, 1, 2, 3)):
        if self.n == 8:
            blocks = [own, self.swap(own, 4, 2), self.swap(own, 2, 4), self.swap(own, 6)]
            for i in places if behind else ():
                blocks[i] = held(blocks[i], *behind)
            return blocks + [self.swap(b, 1) for b in blocks]
        blocks = own[None]
        step = 1
        while step < self.n:
            blocks = jnp.concatenate([blocks, self.swap(blocks, step)])
            step *= 2
        return [blocks[i] for i in range(self.n)]

    def gather_steps(self, own):
        own = own[None]
        if self.n == 8:
            pair = jnp.concatenate([own, self.swap((yield own), 2, 4)])
            pair = yield pair
            other = self.swap(pair, 4, 2)
            other = yield other
            yield Blocks(
                [pair, other, self.swap(pair, 1), self.swap(other, 1)],
                [(0, 0), (1, 0), (0, 1), (1, 1), (2, 0), (3, 0), (2, 1), (3, 1)],
            )
        else:
            blocks, step = own, 1
            count = 0
            while step < self.n:
                if count < 3:
                    blocks = yield blocks
                count += 1
                blocks = jnp.concatenate([blocks, self.swap(blocks, step)])
                step *= 2
            yield Blocks([blocks], [(0, i) for i in range(self.n)])

    def first(self, keep, send):
        count = self.n // 2
        got = self.swap(send, 1 if self.n == 8 else count)
        total = keep.astype(f32) + got.astype(f32)
        return total.reshape(count, -1, keep.shape[-1])

    def outgoing(self, total):
        return total[total.shape[0] // 2 :].astype(bf16)

    def move(self, total, out):
        count = total.shape[0] // 2
        if self.n == 8:
            return self.swap(out, 2, 4) if count == 2 else self.swap(out, 4, 2)
        return self.swap(out, count)

    def add(self, total, got):
        return total[: total.shape[0] // 2] + got.astype(f32)

    def step(self, total):
        return self.add(total, self.move(total, self.outgoing(total)))

    def finish(self, total):
        while total.shape[0] > 2:
            total = self.step(total)
        return total[0], self.move(total, self.outgoing(total))[0]

    def reduce(self, keep, send):
        return self.finish(self.first(keep, send))

    def trade(self, blocks):
        if self.n == 8:
            return [blocks[0]] + [
                self.swap(blocks[i], self.even[i], self.odd[i]) for i in range(1, self.n)
            ]
        return [blocks[0]] + [self.swap(blocks[i], i) for i in range(1, self.n)]

    def sources(self, me):
        even, odd = [0] * self.n, [0] * self.n
        for i in range(self.n):
            even[i] = self.even[i] if self.even[i] % 2 == 0 else self.odd[i]
            odd[i] = self.odd[i] if self.odd[i] % 2 == 0 else self.even[i]
        table = jnp.where(me % 2 == 1, jnp.array(odd, jnp.int32), jnp.array(even, jnp.int32))
        return me ^ table

    def gather_z(self, own):
        return jnp.stack([own] + [self.swap_z(own, k) for k in range(1, self.m)])

    def reduce_z(self, terms):
        total = terms[0].astype(f32)
        for k in range(1, self.m):
            total = total + self.swap_z(terms[k].astype(bf16), k).astype(f32)
        return total


def held(value, *others):
    return lax.optimization_barrier((value, *others))[0]


def make_body(n, m):
    ring = Ring(n, m)
    rows = D // (n * m)
    bias_w = QKV_W // (n * m)
    pad_rows = -(-(rows + 3) // 16) * 16
    step = m * pad_rows
    all_rows = n * step
    units = FF // n
    unit_pad = -(-units // 128) * 128
    cfg = (n, m, rows, pad_rows)

    in_block_row = jnp.arange(all_rows // 2, dtype=jnp.int32)[:, None] % pad_rows

    def row_terms(left, right, *extra_rows):
        cut = all_rows // 2
        halves = []
        for part in (left[:, :cut], left[:, cut:]):
            terms = dot_rows(part, right)
            for i, row in enumerate(extra_rows):
                terms = jnp.where(in_block_row == rows + 1 + i, row, terms)
            halves.append(terms.astype(bf16))
        return halves

    def z_sum(mine, got):
        total = mine + got.astype(f32)
        return ring.reduce_z(total.reshape(m, pad_rows, total.shape[-1]))

    def feed_in_home(parts):
        cut = jnp.stack([p.reshape(n, rows, 2 * unit_pad) for p in parts], axis=1)
        return lax.all_to_all(cut, "ctx", 0, 0, tiled=True)

    def feed_in_out(got):
        got = got.reshape(n, LAYERS, rows, 2, unit_pad)[..., :units].astype(f32)
        return got.transpose(1, 2, 3, 0, 4).reshape(LAYERS, rows, 2 * FF)

    def body(
        hidden_in,
        positions,
        cotangent,
        attn_gain,
        qkv_weight,
        qkv_bias,
        out_weight,
        mlp_gain,
        in_weight,
        down_weight,
    ):
        me, me_z = lax.axis_index("ctx"), lax.axis_index("wt")
        shard = me * m + me_z
        offsets = ring.offsets(me)
        own_positions = positions[0]
        tokens = own_positions.shape[0]

        def spread(vector, width):
            row = jnp.zeros((1, QKV_W), bf16)
            return lax.dynamic_update_slice(row, vector[None], (0, shard * width))

        def qkv_block(l):
            rest = jnp.zeros((pad_rows - rows - 3, QKV_W), bf16)
            return jnp.concatenate(
                [
                    qkv_weight[l],
                    spread(qkv_bias[l], bias_w),
                    spread(attn_gain[l], rows),
                    spread(mlp_gain[l], rows),
                    rest,
                ]
            )

        def out_block(l):
            return jnp.pad(out_weight[l], ((0, pad_rows - rows), (0, 0)))

        def z_blocks(block):
            return ring.gather_z(block).reshape(step, block.shape[-1])

        def both_block(l):
            return jnp.concatenate([qkv_block(l), out_block(l)], axis=1)

        def z_parts(block):
            return [block] + [ring.swap_z(block, k) for k in range(1, m)]

        def z_join(parts):
            return jnp.concatenate(parts, axis=0)

        targets, sources = me ^ offsets, ring.sources(me)
        parts0 = z_parts(both_block(0))
        down0 = lax.all_gather(held(down_weight[0], *parts0), "wt", axis=0, tiled=True)
        cut = cut_columns(targets, [in_weight[l] for l in range(LAYERS)], units, unit_pad)
        steps0 = ring.gather_steps(held(z_join(parts0), cut[0]))
        own0 = next(steps0)
        traded = ring.trade([held(c, own0) for c in cut])
        pair0 = steps0.send(own0)
        traded[-1] = held(traded[-1], pair0)
        in0_got, in1_got = join_rows(sources, traded)
        in0 = lax.all_gather(held(in0_got, down0), "wt", axis=0, tiled=True)
        both0 = steps0.send(steps0.send(pair0))

        own_row = jnp.tile(own_positions, GROUP)[None]

        half_head = HEAD // 2
        frequency = jnp.exp(
            jnp.arange(half_head, dtype=f32) * (-2.0 * math.log(ROPE_BASE) / HEAD)
        )
        angles = own_positions.astype(f32)[:, None] * frequency[None, :]
        cos = jnp.tile(jnp.cos(angles), (1, 4))
        sin = jnp.tile(jnp.sin(angles), (1, 4))

        column = jnp.arange(all_rows, dtype=jnp.int32)
        in_block = column % pad_rows
        block_owner = ((me ^ offsets[:, None]) * m + (me_z ^ jnp.arange(m))[None, :]).reshape(-1)
        owner = jnp.repeat(block_owner, pad_rows)
        feature = jnp.where(in_block < rows, owner * rows + in_block, -1)
        every = jnp.arange(D, dtype=jnp.int32)
        perm = (every[:, None] == feature[None, :]).astype(bf16)
        second, first, inside = every // (n * rows), (every // rows) % n, every % rows
        perm2 = (every[:, None] == ((first * m + second) * rows + inside)[None, :]).astype(bf16)

        lane = jnp.arange(128, dtype=jnp.int32)[None]
        places = jnp.where(
            lane == 0, own_positions[:, None] // 256, jnp.where(lane == 1, own_positions[:, None] % 256, 0)
        ).astype(bf16)

        hidden0, rel0, query0, kv0, gain0 = before_attention(
            cfg, hidden_in[0], [], perm, cos, sin, both0, places
        )
        kvs0 = ring.gather(kv0)
        middle0, normed0, heads0, mix0, lse0, turn0 = attention(
            cfg, query0, kvs0, own_row, kvs0, hidden0, gain0, perm, perm2, both0, QKV_W
        )
        xs0 = ring.gather(normed0)
        steps1 = ring.gather_steps(z_join(z_parts(held(both_block(1), normed0))))
        own1 = next(steps1)
        xs0[-1] = held(xs0[-1], own1)
        keep, send, x_all0, units0, act0 = feed_forward(xs0, in0, down0)
        pair1 = held(steps1.send(own1), keep)
        in1 = lax.all_gather(held(in1_got, in0, xs0[1]), "wt", axis=0, tiled=True)
        total = ring.first(keep, send)
        while total.shape[0] > 2:
            total = ring.step(total)
        out = ring.outgoing(total)
        sums = (total[0], ring.move(total, out)[0])
        both1 = steps1.send(held(steps1.send(pair1), out))
        hidden1, rel1, query1, kv1, gain1 = before_attention(
            cfg, middle0, list(sums), perm, cos, sin, both1
        )
        kvs1 = ring.gather(kv1)
        down1_own = held(down_weight[1], in1, *kvs1)
        cotangent_late = held(cotangent[0], *kvs1)
        down1 = lax.all_gather(down1_own, "wt", axis=0, tiled=True)
        middle1, normed1, heads1, mix1, lse1, turn1 = attention(
            cfg, held(query1, down1_own, cotangent_late), kvs1, own_row, kvs0, hidden1, gain1, perm, perm2, both1, QKV_W
        )
        grads1 = ring.gather(cotangent_late, normed1)
        xs1 = ring.gather(normed1)

        def feed_reduce(keep, send, x_all, ugrad, act, g_all, *sc_behind):
            total = ring.first(keep, send)
            out = ring.outgoing(total)
            got = ring.move(total, out)
            in_terms = dot_rows(held(x_all, out), ugrad).astype(bf16)
            in_part = lax.psum_scatter(
                held(in_terms, *sc_behind), "wt", scatter_dimension=0, tiled=True
            )
            total = ring.add(total, held(got, in_terms))
            while total.shape[0] > 2:
                total = ring.step(total)
            out = ring.outgoing(total)
            got = ring.move(total, out)[0]
            down_terms = dot_rows(held(act, out), g_all)[:units].astype(bf16)
            return (total[0], held(got, down_terms)), in_part, down_terms

        keep, send, g_all1, ugrad1, x_all1, act1 = feed_forward_back(xs1, None, grads1, in1, down1)
        sums, in_part1, down_terms1 = feed_reduce(keep, send, x_all1, ugrad1, act1, g_all1)
        down_part1 = lax.psum_scatter(down_terms1, "wt", scatter_dimension=0, tiled=True)
        mgrad1, low1, mlp_gain_grad1, heads_grad1 = middle_back(
            cfg, sums, middle1, cotangent[0], gain1, perm, perm2, both1, QKV_W
        )
        keep, send, part1 = attention_back(
            cfg, heads_grad1, mix1, lse1, turn1, query1, kvs1, own_row, kvs0, cos, sin
        )
        kv_total = ring.first(keep, send)
        kv_out = ring.outgoing(kv_total)
        kv_got = ring.move(kv_total, kv_out)
        query_rel1 = query_back(cfg, held(part1, kv_out), both1)
        kv_sums = ring.finish(ring.add(kv_total, held(kv_got, query_rel1)))
        kv_sums = (kv_sums[0], held(kv_sums[1], in_part1))
        grad1, grad1_low, kv_part1, attn_gain_grad1 = layer_back(
            cfg, kv_sums, query_rel1, hidden1, mgrad1, gain1, cos, sin, perm, both1
        )
        grads0 = ring.gather(grad1_low, down_part1, places=(3,))

        def wide_row(row):
            return jnp.pad(row[:1], ((0, 0), (0, QKV_W - D)))

        out_keep1, out_send1 = row_terms(heads1, held(low1, grad1_low))
        joint_keep1, joint_send1 = row_terms(
            rel1,
            jnp.concatenate([part1, kv_part1], axis=1),
            wide_row(attn_gain_grad1),
            wide_row(mlp_gain_grad1),
        )
        total1 = jnp.concatenate(
            [ring.first(out_keep1, out_send1), ring.first(joint_keep1, joint_send1)], axis=2
        )
        out1 = ring.outgoing(total1)
        cut = n // 2 * tokens
        act_late = held(act1, joint_send1)[:, :units]
        last_keep = dot(act_late[:cut], down1).astype(bf16)
        last_send = dot(act_late[cut:], down1).astype(bf16)
        hidden_total = ring.first(last_keep, last_send)
        hidden_out1 = ring.outgoing(hidden_total)
        grads0[-1] = held(grads0[-1], out1, hidden_out1)
        keep, send, g_all0, ugrad0 = feed_forward_back(None, units0, grads0, in0, down0)
        got1 = ring.move(total1, out1)
        hidden_got = ring.move(hidden_total, hidden_out1)
        sums, in_part0, down_terms0 = feed_reduce(
            keep, held(send, got1, hidden_got), x_all0, ugrad0, act0, g_all0, down_part1
        )
        mgrad0, low0, mlp_gain_grad0, heads_grad0 = middle_back(
            cfg, sums, middle0, grad1, gain0, perm, perm2, both0, QKV_W
        )
        total1 = ring.add(total1, held(got1, heads_grad0))
        while total1.shape[0] > 2:
            total1 = ring.step(total1)
        out1 = ring.outgoing(total1)
        hidden_total = ring.add(hidden_total, held(hidden_got, heads_grad0))
        while hidden_total.shape[0] > 2:
            hidden_total = ring.step(hidden_total)
        hidden_out1 = ring.outgoing(hidden_total)
        keep, send, part0 = attention_back(
            cfg, held(heads_grad0, out1, hidden_out1), mix0, lse0, turn0, query0, kvs0,
            own_row, kvs0, cos, sin,
        )
        got1 = ring.move(total1, out1)[0]
        hidden_got = ring.move(hidden_total, hidden_out1)[0]
        send = held(send, got1, hidden_got)
        kv_total = ring.first(keep, send)
        kv_out = ring.outgoing(kv_total)
        kv_got = ring.move(kv_total, kv_out)
        query_rel0 = query_back(cfg, held(part0, kv_out), both0)
        out_keep0, out_send0 = row_terms(heads0, held(low0, kv_out), mlp_gain_grad0[:1])
        kv_total = ring.add(kv_total, held(kv_got, query_rel0, out_send0))
        while kv_total.shape[0] > 2:
            kv_total = ring.step(kv_total)
        kv_out = ring.outgoing(kv_total)
        kv_got = ring.move(kv_total, kv_out)[0]
        query_keep0, query_send0 = row_terms(rel0, held(part0, kv_out))
        kv_sums = (kv_total[0], held(kv_got, query_send0))
        first0 = jnp.concatenate(
            [
                ring.first(out_keep0, out_send0),
                held(ring.first(query_keep0, query_send0), *kv_sums),
            ],
            axis=2,
        )
        first_out0 = ring.outgoing(first0)
        first_got0 = ring.move(first0, first_out0)
        down_part0 = lax.psum_scatter(down_terms0, "wt", scatter_dimension=0, tiled=True)
        z_out1 = (total1[0] + held(got1, kv_got).astype(f32)).astype(bf16)
        z_out1 = z_out1.reshape(m, pad_rows, z_out1.shape[-1])
        z_got1 = [ring.swap_z(z_out1[k], k) for k in range(1, m)]
        grad0, unused, kv_part0, attn_gain_grad0 = layer_back(
            cfg, (kv_sums[0], held(kv_sums[1], first_out0, in_part0, z_out1)), query_rel0, hidden0, mgrad0, gain0, cos, sin, perm, both0
        )
        hidden_out = middle1 + hidden_total[0] + held(hidden_got, grad0).astype(f32)
        first0 = ring.add(first0, first_got0)
        gain_rows = jnp.pad(attn_gain_grad0[:1], ((0, 127), (0, 0))).astype(bf16)
        columns = lax.dot_general(
            perm, gain_rows, (((0,), (1,)), ((), ())), preferred_element_type=f32
        ).astype(bf16)
        cut = all_rows // 2
        kv_keep0, kv_send0 = [
            jnp.concatenate([half, columns[i * cut : (i + 1) * cut]], axis=1)
            for i, half in enumerate(row_terms(rel0, kv_part0))
        ]
        last0 = ring.first(kv_keep0, kv_send0)
        last_out0 = ring.outgoing(last0)
        last_got0 = ring.move(last0, last_out0)
        home = feed_in_home([held(in_part0, last_got0), in_part1])
        last0 = ring.add(last0, last_got0)
        total0 = jnp.concatenate([first0, last0], axis=2)
        while total0.shape[0] > 2:
            total0 = ring.step(total0)
        last_got0 = ring.move(total0, held(ring.outgoing(total0), down_part0))[0]
        last_sum0 = (total0[0] + last_got0.astype(f32)).astype(bf16)
        layer0 = ring.reduce_z(last_sum0.reshape(m, pad_rows, last_sum0.shape[-1]))
        layer1 = sum((held(g, layer0).astype(f32) for g in z_got1), z_out1[0].astype(f32))
        gain_at = QW + QKV_W

        def own_part(row, width):
            return lax.dynamic_slice(row, (0, shard * width), (1, width))[0]

        stacked = [
            jnp.stack([layer0[:rows, gain_at], own_part(layer1[rows + 1 : rows + 2, QW:], rows)]),
            jnp.stack([layer[:rows, QW : QW + QKV_W] for layer in (layer0, layer1)]),
            jnp.stack(
                [own_part(l[rows : rows + 1, QW : QW + QKV_W], bias_w) for l in (layer0, layer1)]
            ),
            jnp.stack([layer[:rows, :QW] for layer in (layer0, layer1)]),
            jnp.stack(
                [
                    own_part(layer0[rows + 1 : rows + 2, :QW], rows),
                    own_part(layer1[rows + 2 : rows + 3, QW:], rows),
                ]
            ),
        ]
        in_weight_grad = feed_in_out(held(home, last_sum0))
        down_weight_grad = jnp.stack([down_part0, down_part1]).astype(f32)
        return (hidden_out[None], grad0[None], *stacked, in_weight_grad, down_weight_grad)

    return body


def solution(mesh):
    sizes = dict(mesh.shape)
    rows = P("wt", "ctx", None)
    vector = P(None, ("ctx", "wt"))
    matrix = P(None, ("ctx", "wt"), None)
    return jax.shard_map(
        make_body(sizes["ctx"], sizes["wt"]),
        mesh=mesh,
        in_specs=(
            rows, P("wt", "ctx"), rows, vector, matrix, vector, matrix, vector, matrix, matrix,
        ),
        out_specs=(rows, rows, vector, matrix, vector, matrix, vector, matrix, matrix),
        check_vma=False,
    )
```

```python
import functools
import math

import jax
import jax.numpy as jnp
from jax import lax
from jax.experimental import pallas as pl
from jax.experimental.pallas import tpu as pltpu
from jax.sharding import PartitionSpec as P

HEADS = 14
KV_HEADS = 2
GROUP = HEADS // KV_HEADS
HEAD = 64
FF = 4864
LAYERS = 2
QW = 896
D = 896
QKV_W = 1152
KV_W = KV_HEADS * HEAD

EPSILON = 1e-06
ROPE_BASE = 1000000.0
NEGATIVE = -1e30
SCALE = HEAD**-0.5

bf16 = jnp.bfloat16
f32 = jnp.float32

ANY = pl.BlockSpec(memory_space=pl.ANY)
VMEM = pl.BlockSpec(memory_space=pltpu.VMEM)
DMA = pltpu.SemaphoreType.DMA


def shape(dims, dtype):
    return jax.ShapeDtypeStruct(dims, dtype)


def dot(left, right):
    return jnp.dot(left, right, preferred_element_type=f32)


def dot_rows(left, right):
    return lax.dot_general(left, right, (((0,), (0,)), ((), ())), preferred_element_type=f32)


def dot_cols(left, right):
    return lax.dot_general(left, right, (((1,), (1,)), ((), ())), preferred_element_type=f32)


class Lazy:
    def __init__(self, ref, copy):
        self.ref, self.copy = ref, copy

    def __getitem__(self, at):
        if self.copy is not None:
            self.copy.wait()
            self.copy = None
        return self.ref[at]


class Late:
    def __init__(self, ref, target, sem):
        self.ref, self.copy = ref, pltpu.make_async_copy(ref, target, sem)
        self.sent = False

    def __getitem__(self, at):
        return self.ref[at]

    def __setitem__(self, at, value):
        self.ref[at] = value

    def flush(self):
        self.copy.start()
        self.sent = True


def lazily(kernel, ins, in_specs, outs, out_specs, scratch):
    n_in, n_out = len(ins), len(outs)
    staged = [i for i, spec in enumerate(in_specs) if spec is VMEM]
    late = [i for i, spec in enumerate(out_specs) if spec is VMEM]
    n_scratch = len(scratch)

    def whole(*refs):
        refs = list(refs)
        own = refs[n_in + n_out + n_scratch :]
        ins_v, outs_v = own[: len(staged)], own[len(staged) : len(staged) + len(late)]
        in_sems, out_sems = own[-2:]
        for k, i in enumerate(staged):
            copy = pltpu.make_async_copy(refs[i], ins_v[k], in_sems.at[k])
            copy.start()
            refs[i] = Lazy(ins_v[k], copy)
        results = []
        for k, i in enumerate(late):
            results.append(Late(outs_v[k], refs[n_in + i], out_sems.at[k]))
            refs[n_in + i] = results[-1]
        kernel(*refs[: n_in + n_out + n_scratch])
        for i in staged:
            if refs[i].copy is not None:
                refs[i].copy.wait()
        for result in results:
            if not result.sent:
                result.flush()
        for result in results:
            result.copy.wait()

    scratch = [
        *scratch,
        *[pltpu.VMEM(ins[i].shape, ins[i].dtype) for i in staged],
        *[pltpu.VMEM(outs[i].shape, outs[i].dtype) for i in late],
        DMA((max(len(staged), 1),)),
        DMA((max(len(late), 1),)),
    ]
    in_specs = [ANY if spec is VMEM else spec for spec in in_specs]
    out_specs = [ANY if spec is VMEM else spec for spec in out_specs]
    return whole, in_specs, out_specs, scratch


def run(kernel, ins, in_specs, outs, out_specs, scratch, flops, vmem=60, lazy=False):
    if lazy:
        kernel, in_specs, out_specs, scratch = lazily(
            kernel, ins, in_specs, outs, out_specs, scratch
        )
    moved = sum(math.prod(x.shape) * x.dtype.itemsize for x in [*ins, *outs])
    return pl.pallas_call(
        kernel,
        out_shape=outs,
        in_specs=in_specs,
        out_specs=out_specs,
        scratch_shapes=scratch,
        compiler_params=pltpu.CompilerParams(vmem_limit_bytes=vmem * 2**20),
        cost_estimate=pl.CostEstimate(flops=flops, bytes_accessed=moved, transcendentals=0),
    )(*ins)


def copies(sources, targets, sems):
    made = [pltpu.make_async_copy(s, t, sems.at[i]) for i, (s, t) in enumerate(zip(sources, targets))]
    for c in made:
        c.start()
    return made


def rows_of(ref, count, size):
    return [ref.at[pl.ds(i * size, size)] for i in range(count)]


class Blocks:
    def __init__(self, arrays, places):
        self.arrays, self.places = arrays, places

    def take(self, it):
        refs = [next(it) for _ in self.arrays]
        return [refs[a].at[b] for a, b in self.places]


def turned(block):
    lane = lax.broadcasted_iota(jnp.int32, block.shape, 1)
    return jnp.where(lane % HEAD < HEAD // 2, -pltpu.roll(block, 96, 1), pltpu.roll(block, 32, 1))


def rotated(block, cos, sin):
    return block * cos + turned(block) * sin


def rotated_back(block, cos, sin):
    return block * cos - turned(block) * sin


def inverse_norm(hidden):
    return lax.rsqrt(jnp.mean(hidden * hidden, axis=-1, keepdims=True) + EPSILON)


def norm_back(normed_grad, hidden, gain):
    inverse = inverse_norm(hidden)
    scaled = normed_grad * gain
    inner = jnp.mean(scaled * hidden, axis=-1, keepdims=True)
    into = inverse * scaled - hidden * (inverse * inverse * inverse * inner)
    return into, jnp.sum(normed_grad * (hidden * inverse), axis=0, keepdims=True)


def split_dot_cols(value, right):
    high = value.astype(bf16)
    low = (value - high.astype(f32)).astype(bf16)
    return dot_cols(high, right) + dot_cols(low, right)


def first_row(row):
    return jnp.broadcast_to(row, (8, row.shape[1]))


def before_attention(cfg, base, sums, perm, cos, sin, blocks, places=None):
    n, m, rows, pad_rows = cfg
    tokens, step = base.shape[0], m * pad_rows
    all_rows = n * step
    more = [] if places is None else [places]

    def kernel(*refs):
        it = iter(refs)
        more_refs = [next(it) for _ in more]
        base_ref = next(it)
        sum_refs = [next(it) for _ in sums]
        perm_ref, cos_ref, sin_ref = next(it), next(it), next(it)
        block_refs = blocks.take(it)
        hidden_ref, rel_ref, query_ref, kv_ref, gain_ref, weight, sems = it
        waits = copies(
            [b.at[:, pl.ds(0, QKV_W)] for b in block_refs], rows_of(weight, n, step), sems
        )
        hidden = base_ref[...].astype(f32)
        for ref in sum_refs:
            hidden = hidden + ref[...].astype(f32)
        hidden_ref[...] = hidden
        scaled = hidden * inverse_norm(hidden)
        cos, sin = cos_ref[...], sin_ref[...]
        for w in waits:
            w.wait()
        last = jnp.zeros((16, QKV_W), f32)
        for i in range(n * m):
            last = last + weight[pl.ds((i + 1) * pad_rows - 16, 16), :].astype(f32)
        at = rows + 1 - (pad_rows - 16)
        gain_ref[0:8, :] = first_row(last[at : at + 1, :D])
        gain_ref[8:16, :] = first_row(last[at + 1 : at + 2, :D])
        normed = (scaled * last[at : at + 1, :D]).astype(bf16)
        rel = dot(normed, perm_ref[...])
        lane = lax.broadcasted_iota(jnp.int32, rel.shape, 1)
        rel = jnp.where(lane % pad_rows == rows, 1.0, rel).astype(bf16)
        rel_ref[...] = rel
        kv = dot(rel, weight[:, QW:])
        kv_ref[:, :KV_W] = rotated(kv[:, :KV_W], cos, sin).astype(bf16)
        kv_ref[:, KV_W : 2 * KV_W] = kv[:, KV_W:].astype(bf16)
        for ref in more_refs:
            kv_ref[:, 2 * KV_W :] = ref[...]
        query = dot(rel, weight[:, :QW])
        for i in range(QW // 128):
            part = rotated(query[:, i * 128 : (i + 1) * 128], cos, sin).astype(bf16)
            query_ref[:, i * 128 : (i + 1) * 128] = part * SCALE

    ins = [*more, base, *sums, perm, cos, sin]
    return run(
        kernel,
        [*ins, *blocks.arrays],
        [VMEM] * len(ins) + [ANY] * len(blocks.arrays),
        [
            shape((tokens, D), f32),
            shape((tokens, all_rows), bf16),
            shape((tokens, QW), bf16),
            shape((tokens, 2 * KV_W + 128 * len(more)), bf16),
            shape((16, D), f32),
        ],
        [VMEM] * 5,
        [pltpu.VMEM((all_rows, QKV_W), bf16), DMA((n,))],
        2 * tokens * all_rows * (D + QKV_W),
    )


def kv_copies(n, tokens, kv_refs, place_refs, kv, place, sems):
    return copies(
        [
            *[r.at[:, pl.ds(0, 2 * KV_W)] for r in kv_refs],
            *[r.at[:, pl.ds(2 * KV_W, 128)] for r in place_refs],
        ],
        [*rows_of(kv, n, tokens), *rows_of(place, n, tokens)],
        sems,
    )


def place_column(place, at):
    block = place[at, :].astype(f32)
    return (block[:, 0:1] * 256.0 + block[:, 1:2]).astype(jnp.int32)


def heads_to_lanes(matrix, group, tokens):
    parts = [
        matrix[(group * GROUP + h) * HEAD : (group * GROUP + h + 1) * HEAD, :] for h in range(GROUP)
    ]
    return jnp.concatenate(parts, axis=1)


def lanes_to_heads(groups, tokens):
    parts = [g[:, h * tokens : (h + 1) * tokens] for g in groups for h in range(GROUP)]
    return jnp.concatenate(parts, axis=0).T


def heads_to_rows(matrix, group):
    parts = [
        matrix[:, (group * GROUP + h) * HEAD : (group * GROUP + h + 1) * HEAD] for h in range(GROUP)
    ]
    return jnp.concatenate(parts, axis=0)


def attention(
    cfg, query, kv_blocks, own_row, place_blocks, hidden, gain, perm, perm2, out_blocks, out_at
):
    n, m, rows, pad_rows = cfg
    tokens, step = query.shape[0], m * pad_rows
    all_rows, wide = n * step, GROUP * query.shape[0]
    slots = KV_HEADS if n <= 8 else 1

    def kernel(*refs):
        it = iter(refs)
        query_ref = next(it)
        kv_refs = [next(it) for _ in range(n)]
        place_refs = [next(it) for _ in range(n)]
        row_ref, hidden_ref, gain_ref, perm_in, perm2_in = [next(it) for _ in range(5)]
        out_refs = out_blocks.take(it)
        middle_ref, normed_ref, rel_ref, mix_ref, lse_ref, turn_ref = [next(it) for _ in range(6)]
        kv, place, values_t, scores = [next(it) for _ in range(4)]
        probs = next(it) if slots > 1 else None
        perm_v, perm2_v, weight, kv_sems, sems = it
        kv_waits = kv_copies(n, tokens, kv_refs, place_refs, kv, place, kv_sems)
        waits = copies(
            [perm_in, perm2_in, *[o.at[:, pl.ds(out_at, D)] for o in out_refs]],
            [perm_v, perm2_v, *rows_of(weight, n, step)],
            sems,
        )
        query_t = query_ref[...].astype(f32).T
        for w in kv_waits:
            w.wait()
        for g in range(KV_HEADS):
            turn_ref[g * HEAD : (g + 1) * HEAD, :] = heads_to_lanes(query_t, g, tokens).astype(bf16)

        if probs is None:
            for j in range(n):
                block = kv[pl.ds(j * tokens, tokens), KV_W:]
                values_t[j] = block.astype(f32).T.astype(bf16)
        else:
            values_t[...] = kv[:, KV_W:].astype(f32).T.astype(bf16)
        own = row_ref[...]
        mixed = []
        for g in range(KV_HEADS):
            turn = turn_ref[g * HEAD : (g + 1) * HEAD, :]
            top = jnp.full((1, wide), NEGATIVE, f32)
            for j in range(n):
                at = pl.ds(j * tokens, tokens)
                s = dot(kv[at, g * HEAD : (g + 1) * HEAD], turn)
                s = jnp.where(place_column(place, at) <= own, s, NEGATIVE)
                scores[g % slots, at, :] = s
                top = jnp.maximum(top, jnp.max(s, axis=0, keepdims=True))
            total = jnp.zeros((1, wide), f32)
            out = jnp.zeros((HEAD, wide), f32)
            for j in range(n):
                at = pl.ds(j * tokens, tokens)
                p = jnp.exp(scores[g % slots, at, :] - top)
                total = total + jnp.sum(p, axis=0, keepdims=True)
                if probs is None:
                    out = out + dot(values_t[j, g * HEAD : (g + 1) * HEAD, :], p.astype(bf16))
                else:
                    probs[g, at, :] = p.astype(bf16)
            if probs is not None:
                out = dot(values_t[g * HEAD : (g + 1) * HEAD, :], probs[g])
            out = out / total
            mix_ref[g * HEAD : (g + 1) * HEAD, :] = out
            lse_ref[g * 8 : (g + 1) * 8, :] = first_row(top + jnp.log(total))
            mixed.append(out)
        heads = lanes_to_heads(mixed, tokens).astype(bf16)
        for w in waits:
            w.wait()
        rel = dot(heads, perm_v[...]).astype(bf16)
        rel_ref[...] = rel
        middle = hidden_ref[...] + dot(rel, weight[...])
        middle_ref[...] = middle
        normed = (middle * inverse_norm(middle) * gain_ref[8:9, :]).astype(bf16)
        normed_ref[...] = dot(normed, perm2_v[...]).astype(bf16)

    return run(
        kernel,
        [query, *kv_blocks, *place_blocks, own_row, hidden, gain, perm, perm2, *out_blocks.arrays],
        [VMEM] + [ANY] * (2 * n) + [VMEM] * 3 + [ANY] * (len(out_blocks.arrays) + 2),
        [
            shape((tokens, D), f32),
            shape((tokens, D), bf16),
            shape((tokens, all_rows), bf16),
            shape((KV_W, wide), f32),
            shape((16, wide), f32),
            shape((KV_W, wide), bf16),
        ],
        [VMEM] * 6,
        [
            pltpu.VMEM((n * tokens, 2 * KV_W), bf16),
            pltpu.VMEM((n * tokens, 128), bf16),
            pltpu.VMEM((KV_W, n * tokens) if slots > 1 else (n, KV_W, tokens), bf16),
            pltpu.VMEM((slots, n * tokens, wide), f32),
            *([pltpu.VMEM((slots, n * tokens, wide), bf16)] if slots > 1 else []),
            pltpu.VMEM((D, all_rows), bf16),
            pltpu.VMEM((D, D), bf16),
            pltpu.VMEM((all_rows, D), bf16),
            DMA((2 * n,)),
            DMA((n + 2,)),
        ],
        8 * tokens * n * tokens * QW,
        60,
    )


def middle_back(cfg, sums, middle, gradient, gain, perm, perm2, out_blocks, out_at):
    n, m, rows, pad_rows = cfg
    tokens, step = middle.shape[0], m * pad_rows
    all_rows = n * step

    def kernel(*refs):
        it = iter(refs)
        sum_refs = [next(it), next(it)]
        middle_ref, grad_ref, gain_ref, perm_in, perm2_ref = [next(it) for _ in range(5)]
        out_refs = out_blocks.take(it)
        mgrad_ref, low_ref, gain_grad_ref, heads_ref = [next(it) for _ in range(4)]
        perm_v, weight, sems = it
        waits = copies(
            [perm_in, *[o.at[:, pl.ds(out_at, D)] for o in out_refs]],
            [perm_v, *rows_of(weight, n, step)],
            sems,
        )
        normed_grad = split_dot_cols(
            sum_refs[0][...] + sum_refs[1][...].astype(f32), perm2_ref[...]
        )
        into, gain_grad = norm_back(normed_grad, middle_ref[...], gain_ref[8:9, :])
        middle_grad = grad_ref[...].astype(f32) + into
        mgrad_ref[...] = middle_grad
        gain_grad_ref[...] = first_row(gain_grad)
        low = middle_grad.astype(bf16)
        low_ref[...] = low
        for w in waits:
            w.wait()
        heads_rel = dot_cols(low, weight[...]).astype(bf16)
        heads_ref[...] = dot_cols(heads_rel, perm_v[...]).astype(bf16)

    return run(
        kernel,
        [*sums, middle, gradient, gain, perm, perm2, *out_blocks.arrays],
        [VMEM] * 5 + [ANY] + [VMEM] + [ANY] * len(out_blocks.arrays),
        [
            shape((tokens, D), f32),
            shape((tokens, D), bf16),
            shape((8, D), f32),
            shape((tokens, QW), bf16),
        ],
        [VMEM] * 4,
        [pltpu.VMEM((D, all_rows), bf16), pltpu.VMEM((all_rows, D), bf16), DMA((n + 1,))],
        2 * tokens * D * (2 * D + 2 * all_rows),
    )


def attention_back(
    cfg, heads_grad, mix, lse, turn, query, kv_blocks, own_row, place_blocks, cos, sin
):
    n, m, rows, pad_rows = cfg
    tokens, half = query.shape[0], n // 2
    wide = GROUP * query.shape[0]

    def kernel(*refs):
        it = iter(refs)
        heads_ref, mix_ref, lse_ref, turn_ref, query_ref = [next(it) for _ in range(5)]
        kv_refs = [next(it) for _ in range(n)]
        place_refs = [next(it) for _ in range(n)]
        row_ref, cos_ref, sin_ref = [next(it) for _ in range(3)]
        keep_ref, send_ref, part_ref = [next(it) for _ in range(3)]
        kv, place, keys_t, probs, score_grads, kv_sems = it
        kv_waits = kv_copies(n, tokens, kv_refs, place_refs, kv, place, kv_sems)
        heads = heads_ref[...]
        heads_t = heads.astype(f32).T
        for w in kv_waits:
            w.wait()
        keys_t[...] = kv[:, :KV_W].astype(f32).T.astype(bf16)
        own = row_ref[...]
        query = query_ref[...]
        sides = []
        for g in range(KV_HEADS):
            grad_t = heads_to_lanes(heads_t, g, tokens)
            inner = jnp.sum(mix_ref[g * HEAD : (g + 1) * HEAD, :] * grad_t, axis=0, keepdims=True)
            sides.append(
                (
                    turn_ref[g * HEAD : (g + 1) * HEAD, :],
                    heads_to_rows(query, g),
                    grad_t.astype(bf16),
                    heads_to_rows(heads, g),
                    inner,
                    lse_ref[g * 8 : g * 8 + 1, :],
                )
            )
        wholes = []
        for g, (turn, query_rows, grad_t, grad_rows, inner, lse) in enumerate(sides):
            for j in range(n):
                at = pl.ds(j * tokens, tokens)
                s = dot(kv[at, g * HEAD : (g + 1) * HEAD], turn)
                p = jnp.exp(jnp.where(place_column(place, at) <= own, s, NEGATIVE) - lse)
                prob_grad = dot(kv[at, KV_W + g * HEAD : KV_W + (g + 1) * HEAD], grad_t)
                probs[at, :] = p.astype(bf16)
                score_grads[at, :] = (p * (prob_grad - inner)).astype(bf16)
            for part, ref in enumerate([keep_ref, send_ref]):
                at = pl.ds(part * half * tokens, half * tokens)
                key_out = dot(score_grads[at, :], query_rows).astype(bf16)
                value_out = dot(probs[at, :], grad_rows).astype(bf16)
                ref[:, g * HEAD : (g + 1) * HEAD] = key_out
                ref[:, KV_W + g * HEAD : KV_W + (g + 1) * HEAD] = value_out
            wholes.append(dot(keys_t[g * HEAD : (g + 1) * HEAD, :], score_grads[...]))
        keep_ref.flush()
        send_ref.flush()
        whole = lanes_to_heads(wholes, tokens) * SCALE
        cos, sin = cos_ref[...], sin_ref[...]
        for i in range(QW // 128):
            at = slice(i * 128, (i + 1) * 128)
            part_ref[:, at] = rotated_back(whole[:, at], cos, sin).astype(bf16)

    return run(
        kernel,
        [heads_grad, mix, lse, turn, query, *kv_blocks, *place_blocks, own_row, cos, sin],
        [VMEM] * 5 + [ANY] * (2 * n) + [VMEM] * 3,
        [
            shape((half * tokens, 2 * KV_W), bf16),
            shape((half * tokens, 2 * KV_W), bf16),
            shape((tokens, QW), bf16),
        ],
        [VMEM] * 3,
        [
            pltpu.VMEM((n * tokens, 2 * KV_W), bf16),
            pltpu.VMEM((n * tokens, 128), bf16),
            pltpu.VMEM((KV_W, n * tokens), bf16),
            pltpu.VMEM((n * tokens, wide), bf16),
            pltpu.VMEM((n * tokens, wide), bf16),
            DMA((2 * n,)),
        ],
        20 * tokens * n * tokens * QW,
        60,
        lazy=True,
    )


def query_back(cfg, query_part, blocks):
    n, m, rows, pad_rows = cfg
    tokens, step = query_part.shape[0], m * pad_rows

    def kernel(*refs):
        it = iter(refs)
        part_ref, block_refs = next(it), blocks.take(it)
        out_ref, weight, sems = it
        waits = copies(
            [b.at[:, pl.ds(0, QW)] for b in block_refs], rows_of(weight, n, step), sems
        )
        for w in waits:
            w.wait()
        out_ref[...] = dot_cols(part_ref[...], weight[...])

    return run(
        kernel,
        [query_part, *blocks.arrays],
        [VMEM] + [ANY] * len(blocks.arrays),
        [shape((tokens, n * step), f32)],
        [VMEM],
        [pltpu.VMEM((n * step, QW), bf16), DMA((n,))],
        2 * tokens * n * step * QW,
        lazy=True,
    )[0]


def layer_back(cfg, sums, query_rel, hidden, middle_grad, gain, cos, sin, perm, blocks):
    n, m, rows, pad_rows = cfg
    tokens, step = hidden.shape[0], m * pad_rows

    def kernel(*refs):
        it = iter(refs)
        sum_refs = [next(it), next(it)]
        rel_ref, hidden_ref, mgrad_ref, gain_ref, cos_ref, sin_ref, perm_ref = [
            next(it) for _ in range(7)
        ]
        block_refs = blocks.take(it)
        grad_ref, low_ref, part_ref, gain_grad_ref, weight, sems = it
        waits = copies(
            [b.at[:, pl.ds(QW, 2 * KV_W)] for b in block_refs], rows_of(weight, n, step), sems
        )
        total = sum_refs[0][...] + sum_refs[1][...].astype(f32)
        keys = rotated_back(total[:, :KV_W], cos_ref[...], sin_ref[...])
        part = jnp.concatenate([keys, total[:, KV_W:]], axis=1).astype(bf16)
        part_ref[...] = part
        part_ref.flush()
        for w in waits:
            w.wait()
        rel = rel_ref[...] + dot_cols(part, weight[...])
        normed_grad = split_dot_cols(rel, perm_ref[...])
        into, gain_grad = norm_back(normed_grad, hidden_ref[...], gain_ref[0:1, :])
        gradient = mgrad_ref[...] + into
        grad_ref[...] = gradient
        low_ref[...] = gradient.astype(bf16)
        gain_grad_ref[...] = first_row(gain_grad)

    return run(
        kernel,
        [*sums, query_rel, hidden, middle_grad, gain, cos, sin, perm, *blocks.arrays],
        [VMEM] * 9 + [ANY] * len(blocks.arrays),
        [
            shape((tokens, D), f32),
            shape((tokens, D), bf16),
            shape((tokens, 2 * KV_W), bf16),
            shape((8, D), f32),
        ],
        [VMEM] * 4,
        [pltpu.VMEM((n * step, 2 * KV_W), bf16), DMA((n,))],
        2 * tokens * n * step * (2 * KV_W + 2 * D),
        lazy=True,
    )


def gated(gate, up):
    return gate * jax.nn.sigmoid(gate) * up


def gated_back(act_grad, gate, up):
    sig = jax.nn.sigmoid(gate)
    gate_grad = act_grad * up * (sig * (1.0 + gate * (1.0 - sig)))
    return gate_grad, act_grad * (gate * sig)


def feed_forward(x_blocks, in_proj, down_proj):
    n, tokens, units, width = len(x_blocks), x_blocks[0].shape[0], down_proj.shape[0], in_proj.shape[1]
    half, pad, total = n // 2, width // 2, n * tokens

    def kernel(*refs):
        x_refs, (in_ref, down_ref) = refs[:n], refs[n : n + 2]
        keep_ref, send_ref, all_ref, unit_ref, act_ref = refs[n + 2 : n + 7]
        x, w_in, w_down, units_v, act_v, terms, x_sems, w_sems, o_sems = refs[n + 7 :]
        in_wait, down_wait = copies([in_ref, down_ref], [w_in, w_down.at[pl.ds(0, units)]], w_sems)
        x_waits = copies(x_refs, rows_of(x, n, tokens), x_sems)
        if pad > units:
            w_down[units:, :] = jnp.zeros((pad - units, D), bf16)
        in_wait.wait()
        down_wait.wait()
        outs = []

        def put(src, dst, slot):
            copy = pltpu.make_async_copy(src, dst, o_sems.at[slot])
            copy.start()
            outs.append(copy)

        big = half * tokens
        for i, (part, target) in enumerate([(1, send_ref), (0, keep_ref)]):
            at = pl.ds(part * big, big)
            for w in x_waits[part * half : (part + 1) * half]:
                w.wait()
            put(x.at[at], all_ref.at[at], 4 * i)
            both = dot(x[at, :], w_in[...])
            units_v[at, :] = both.astype(bf16)
            put(units_v.at[at], unit_ref.at[at], 4 * i + 1)
            act = gated(both[:, :pad], both[:, pad:]).astype(bf16)
            act_v[at, :] = act
            put(act_v.at[at], act_ref.at[at], 4 * i + 2)
            terms[part] = dot(act, w_down[...]).astype(bf16)
            put(terms.at[part], target, 4 * i + 3)
        for copy in outs:
            copy.wait()

    return run(
        kernel,
        [*x_blocks, in_proj, down_proj],
        [ANY] * (n + 2),
        [
            shape((half * tokens, D), bf16),
            shape((half * tokens, D), bf16),
            shape((total, D), bf16),
            shape((total, width), bf16),
            shape((total, pad), bf16),
        ],
        [ANY] * 5,
        [
            pltpu.VMEM((total, D), bf16),
            pltpu.VMEM((D, width), bf16),
            pltpu.VMEM((pad, D), bf16),
            pltpu.VMEM((total, width), bf16),
            pltpu.VMEM((total, pad), bf16),
            pltpu.VMEM((2, half * tokens, D), bf16),
            DMA((n,)),
            DMA((2,)),
            DMA((8,)),
        ],
        2 * total * D * (width + pad),
        60,
    )


def feed_forward_back(x_blocks, units_all, grad_blocks, in_proj, down_proj):
    n, tokens = len(grad_blocks), grad_blocks[0].shape[0]
    units, width = down_proj.shape[0], in_proj.shape[1]
    half, pad, total = n // 2, width // 2, n * tokens
    fresh = units_all is None

    def kernel(*refs):
        it = iter(refs)
        x_refs = [next(it) for _ in range(n)] if fresh else []
        unit_ref = None if fresh else next(it)
        g_refs = [next(it) for _ in range(n)]
        in_ref, down_ref = next(it), next(it)
        keep_ref, send_ref, gall_ref, ugrad_ref = [next(it) for _ in range(4)]
        all_ref, act_ref = (next(it), next(it)) if fresh else (None, None)
        g, w_in, w_down, ugrad, terms = [next(it) for _ in range(5)]
        x, act_v = (next(it), next(it)) if fresh else (None, None)
        units_v = None if fresh else next(it)
        g_sems, w_sems, o_sems, x_sems = it
        in_wait, down_wait = copies([in_ref, down_ref], [w_in, w_down.at[pl.ds(0, units)]], w_sems)
        g_waits = copies(g_refs, rows_of(g, n, tokens), g_sems)
        if fresh:
            x_waits = copies(x_refs, rows_of(x, n, tokens), x_sems)
        else:
            x_waits = copies(rows_of(unit_ref, n, tokens), rows_of(units_v, n, tokens), x_sems)
        if pad > units:
            w_down[units:, :] = jnp.zeros((pad - units, D), bf16)
        in_wait.wait()
        down_wait.wait()
        outs = []

        def put(src, dst, slot):
            copy = pltpu.make_async_copy(src, dst, o_sems.at[slot])
            copy.start()
            outs.append(copy)

        big = half * tokens
        for i, (part, target) in enumerate([(1, send_ref), (0, keep_ref)]):
            at = pl.ds(part * big, big)
            for w in x_waits[part * half : (part + 1) * half]:
                w.wait()
            if fresh:
                put(x.at[at], all_ref.at[at], 5 * i)
                both = dot(x[at, :], w_in[...])
                gate, up = both[:, :pad], both[:, pad:]
                act_v[at, :] = gated(gate, up).astype(bf16)
                put(act_v.at[at], act_ref.at[at], 5 * i + 1)
            else:
                gate, up = units_v[at, :pad].astype(f32), units_v[at, pad:].astype(f32)
            for w in g_waits[part * half : (part + 1) * half]:
                w.wait()
            put(g.at[at], gall_ref.at[at], 5 * i + 2)
            gate_grad, up_grad = gated_back(dot_cols(g[at, :], w_down[...]), gate, up)
            ugrad[at, :pad] = gate_grad.astype(bf16)
            ugrad[at, pad:] = up_grad.astype(bf16)
            put(ugrad.at[at], ugrad_ref.at[at], 5 * i + 3)
            terms[part] = dot_cols(ugrad[at, :], w_in[...]).astype(bf16)
            put(terms.at[part], target, 5 * i + 4)
        for copy in outs:
            copy.wait()

    ins = [*(x_blocks if fresh else [units_all]), *grad_blocks, in_proj, down_proj]
    outs = [
        shape((half * tokens, D), bf16),
        shape((half * tokens, D), bf16),
        shape((total, D), bf16),
        shape((total, width), bf16),
    ]
    scratch = [
        pltpu.VMEM((total, D), bf16),
        pltpu.VMEM((D, width), bf16),
        pltpu.VMEM((pad, D), bf16),
        pltpu.VMEM((total, width), bf16),
        pltpu.VMEM((2, half * tokens, D), bf16),
    ]
    if fresh:
        outs += [shape((total, D), bf16), shape((total, pad), bf16)]
        scratch += [pltpu.VMEM((total, D), bf16), pltpu.VMEM((total, pad), bf16)]
    else:
        scratch += [pltpu.VMEM((total, width), bf16)]
    scratch += [DMA((n,)), DMA((2,)), DMA((10,)), DMA((n,))]
    return run(
        kernel,
        ins,
        [ANY] * len(ins),
        outs,
        [ANY] * len(outs),
        scratch,
        2 * total * D * (width * (2 if fresh else 1) + pad),
        60,
    )


def cut_columns(order, weights, units, unit_pad):
    n, (rows, _), layers = order.shape[0], weights[0].shape, len(weights)

    def kernel(order_ref, *refs):
        weight_refs, outs, parts = refs[:layers], refs[layers:-1], refs[-1]
        zeros = jnp.zeros((rows, unit_pad - units), bf16)
        for l in range(layers):
            for c in range(n):
                for k in range(2):
                    at, to = k * FF + c * units, k * unit_pad
                    parts[c, l, :, to : to + units] = weight_refs[l][:, at : at + units]
                    if unit_pad > units:
                        parts[c, l, :, to + units : to + unit_pad] = zeros
        for a in range(n):
            outs[a][...] = parts[order_ref[a]]

    return run(
        kernel,
        [order, *weights],
        [pl.BlockSpec(memory_space=pltpu.SMEM)] + [VMEM] * layers,
        [shape((layers, rows, 2 * unit_pad), bf16)] * n,
        [VMEM] * n,
        [pltpu.VMEM((n, layers, rows, 2 * unit_pad), bf16)],
        0,
    )


def join_rows(order, blocks):
    n, (layers, rows, width) = len(blocks), blocks[0].shape

    def kernel(order_ref, *refs):
        block_refs, outs, parts = refs[:n], refs[n:-1], refs[-1]
        for a in range(n):
            parts[order_ref[a]] = block_refs[a][...]
        for l in range(layers):
            for c in range(n):
                outs[l][c * rows : (c + 1) * rows, :] = parts[c, l]

    return run(
        kernel,
        [order, *blocks],
        [pl.BlockSpec(memory_space=pltpu.SMEM)] + [VMEM] * n,
        [shape((n * rows, width), bf16)] * layers,
        [VMEM] * layers,
        [pltpu.VMEM((n, layers, rows, width), bf16)],
        0,
    )


class Ring:
    def __init__(self, n, m):
        self.n, self.m = n, m
        if n == 8:
            self.even = [0, 4, 2, 6, 1, 3, 5, 7]
            self.odd = [0, 2, 4, 6, 1, 5, 3, 7]
        else:
            self.even = self.odd = list(range(n))

    def swap(self, value, offset, odd_offset=None):
        odd_offset = offset if odd_offset is None else odd_offset
        return lax.ppermute(
            value, "ctx", [(i, i ^ (odd_offset if i % 2 else offset)) for i in range(self.n)]
        )

    def swap_z(self, value, offset):
        return lax.ppermute(value, "wt", [(i, i ^ offset) for i in range(self.m)])

    def offsets(self, me):
        return jnp.where(
            me % 2 == 1, jnp.array(self.odd, jnp.int32), jnp.array(self.even, jnp.int32)
        )

    def gather(self, own, *behind, places=(0, 1, 2, 3)):
        if self.n == 8:
            blocks = [own, self.swap(own, 4, 2), self.swap(own, 2, 4), self.swap(own, 6)]
            for i in places if behind else ():
                blocks[i] = held(blocks[i], *behind)
            return blocks + [self.swap(b, 1) for b in blocks]
        blocks = own[None]
        step = 1
        while step < self.n:
            blocks = jnp.concatenate([blocks, self.swap(blocks, step)])
            step *= 2
        return [blocks[i] for i in range(self.n)]

    def gather_steps(self, own):
        own = own[None]
        if self.n == 8:
            pair = jnp.concatenate([own, self.swap((yield own), 2, 4)])
            pair = yield pair
            other = self.swap(pair, 4, 2)
            other = yield other
            yield Blocks(
                [pair, other, self.swap(pair, 1), self.swap(other, 1)],
                [(0, 0), (1, 0), (0, 1), (1, 1), (2, 0), (3, 0), (2, 1), (3, 1)],
            )
        else:
            blocks, step = own, 1
            count = 0
            while step < self.n:
                if count < 3:
                    blocks = yield blocks
                count += 1
                blocks = jnp.concatenate([blocks, self.swap(blocks, step)])
                step *= 2
            yield Blocks([blocks], [(0, i) for i in range(self.n)])

    def first(self, keep, send):
        count = self.n // 2
        got = self.swap(send, 1 if self.n == 8 else count)
        total = keep.astype(f32) + got.astype(f32)
        return total.reshape(count, -1, keep.shape[-1])

    def outgoing(self, total):
        return total[total.shape[0] // 2 :].astype(bf16)

    def move(self, total, out):
        count = total.shape[0] // 2
        if self.n == 8:
            return self.swap(out, 2, 4) if count == 2 else self.swap(out, 4, 2)
        return self.swap(out, count)

    def add(self, total, got):
        return total[: total.shape[0] // 2] + got.astype(f32)

    def step(self, total):
        return self.add(total, self.move(total, self.outgoing(total)))

    def finish(self, total):
        while total.shape[0] > 2:
            total = self.step(total)
        return total[0], self.move(total, self.outgoing(total))[0]

    def reduce(self, keep, send):
        return self.finish(self.first(keep, send))

    def trade(self, blocks):
        if self.n == 8:
            return [blocks[0]] + [
                self.swap(blocks[i], self.even[i], self.odd[i]) for i in range(1, self.n)
            ]
        return [blocks[0]] + [self.swap(blocks[i], i) for i in range(1, self.n)]

    def sources(self, me):
        even, odd = [0] * self.n, [0] * self.n
        for i in range(self.n):
            even[i] = self.even[i] if self.even[i] % 2 == 0 else self.odd[i]
            odd[i] = self.odd[i] if self.odd[i] % 2 == 0 else self.even[i]
        table = jnp.where(me % 2 == 1, jnp.array(odd, jnp.int32), jnp.array(even, jnp.int32))
        return me ^ table

    def gather_z(self, own):
        return jnp.stack([own] + [self.swap_z(own, k) for k in range(1, self.m)])

    def reduce_z(self, terms):
        total = terms[0].astype(f32)
        for k in range(1, self.m):
            total = total + self.swap_z(terms[k].astype(bf16), k).astype(f32)
        return total


def held(value, *others):
    return lax.optimization_barrier((value, *others))[0]


def make_body(n, m):
    ring = Ring(n, m)
    rows = D // (n * m)
    bias_w = QKV_W // (n * m)
    pad_rows = -(-(rows + 3) // 16) * 16
    step = m * pad_rows
    all_rows = n * step
    units = FF // n
    unit_pad = -(-units // 128) * 128
    cfg = (n, m, rows, pad_rows)

    in_block_row = jnp.arange(all_rows // 2, dtype=jnp.int32)[:, None] % pad_rows

    def row_terms(left, right, *extra_rows):
        cut = all_rows // 2
        halves = []
        for part in (left[:, :cut], left[:, cut:]):
            terms = dot_rows(part, right)
            for i, row in enumerate(extra_rows):
                terms = jnp.where(in_block_row == rows + 1 + i, row, terms)
            halves.append(terms.astype(bf16))
        return halves

    def z_sum(mine, got):
        total = mine + got.astype(f32)
        return ring.reduce_z(total.reshape(m, pad_rows, total.shape[-1]))

    def feed_in_home(parts):
        cut = jnp.stack([p.reshape(n, rows, 2 * unit_pad) for p in parts], axis=1)
        return lax.all_to_all(cut, "ctx", 0, 0, tiled=True)

    def feed_in_out(got):
        got = got.reshape(n, LAYERS, rows, 2, unit_pad)[..., :units].astype(f32)
        return got.transpose(1, 2, 3, 0, 4).reshape(LAYERS, rows, 2 * FF)

    def body(
        hidden_in,
        positions,
        cotangent,
        attn_gain,
        qkv_weight,
        qkv_bias,
        out_weight,
        mlp_gain,
        in_weight,
        down_weight,
    ):
        me, me_z = lax.axis_index("ctx"), lax.axis_index("wt")
        shard = me * m + me_z
        offsets = ring.offsets(me)
        own_positions = positions[0]
        tokens = own_positions.shape[0]

        def spread(vector, width):
            row = jnp.zeros((1, QKV_W), bf16)
            return lax.dynamic_update_slice(row, vector[None], (0, shard * width))

        def qkv_block(l):
            rest = jnp.zeros((pad_rows - rows - 3, QKV_W), bf16)
            return jnp.concatenate(
                [
                    qkv_weight[l],
                    spread(qkv_bias[l], bias_w),
                    spread(attn_gain[l], rows),
                    spread(mlp_gain[l], rows),
                    rest,
                ]
            )

        def out_block(l):
            return jnp.pad(out_weight[l], ((0, pad_rows - rows), (0, 0)))

        def z_blocks(block):
            return ring.gather_z(block).reshape(step, block.shape[-1])

        def both_block(l):
            return jnp.concatenate([qkv_block(l), out_block(l)], axis=1)

        def z_parts(block):
            return [block] + [ring.swap_z(block, k) for k in range(1, m)]

        def z_join(parts):
            return jnp.concatenate(parts, axis=0)

        targets, sources = me ^ offsets, ring.sources(me)
        parts0 = z_parts(both_block(0))
        down0 = lax.all_gather(held(down_weight[0], *parts0), "wt", axis=0, tiled=True)
        cut = cut_columns(targets, [in_weight[l] for l in range(LAYERS)], units, unit_pad)
        steps0 = ring.gather_steps(held(z_join(parts0), cut[0]))
        own0 = next(steps0)
        traded = ring.trade([held(c, own0) for c in cut])
        pair0 = steps0.send(own0)
        traded[-1] = held(traded[-1], pair0)
        in0_got, in1_got = join_rows(sources, traded)
        in0 = lax.all_gather(held(in0_got, down0), "wt", axis=0, tiled=True)
        both0 = steps0.send(steps0.send(pair0))

        own_row = jnp.tile(own_positions, GROUP)[None]

        half_head = HEAD // 2
        frequency = jnp.exp(
            jnp.arange(half_head, dtype=f32) * (-2.0 * math.log(ROPE_BASE) / HEAD)
        )
        angles = own_positions.astype(f32)[:, None] * frequency[None, :]
        cos = jnp.tile(jnp.cos(angles), (1, 4))
        sin = jnp.tile(jnp.sin(angles), (1, 4))

        column = jnp.arange(all_rows, dtype=jnp.int32)
        in_block = column % pad_rows
        block_owner = ((me ^ offsets[:, None]) * m + (me_z ^ jnp.arange(m))[None, :]).reshape(-1)
        owner = jnp.repeat(block_owner, pad_rows)
        feature = jnp.where(in_block < rows, owner * rows + in_block, -1)
        every = jnp.arange(D, dtype=jnp.int32)
        perm = (every[:, None] == feature[None, :]).astype(bf16)
        second, first, inside = every // (n * rows), (every // rows) % n, every % rows
        perm2 = (every[:, None] == ((first * m + second) * rows + inside)[None, :]).astype(bf16)

        lane = jnp.arange(128, dtype=jnp.int32)[None]
        places = jnp.where(
            lane == 0, own_positions[:, None] // 256, jnp.where(lane == 1, own_positions[:, None] % 256, 0)
        ).astype(bf16)

        hidden0, rel0, query0, kv0, gain0 = before_attention(
            cfg, hidden_in[0], [], perm, cos, sin, both0, places
        )
        kvs0 = ring.gather(kv0)
        middle0, normed0, heads0, mix0, lse0, turn0 = attention(
            cfg, query0, kvs0, own_row, kvs0, hidden0, gain0, perm, perm2, both0, QKV_W
        )
        xs0 = ring.gather(normed0)
        steps1 = ring.gather_steps(z_join(z_parts(held(both_block(1), normed0))))
        own1 = next(steps1)
        xs0[-1] = held(xs0[-1], own1)
        keep, send, x_all0, units0, act0 = feed_forward(xs0, in0, down0)
        pair1 = held(steps1.send(own1), keep)
        in1 = lax.all_gather(held(in1_got, in0, xs0[1]), "wt", axis=0, tiled=True)
        total = ring.first(keep, send)
        while total.shape[0] > 2:
            total = ring.step(total)
        out = ring.outgoing(total)
        sums = (total[0], ring.move(total, out)[0])
        both1 = steps1.send(held(steps1.send(pair1), out))
        hidden1, rel1, query1, kv1, gain1 = before_attention(
            cfg, middle0, list(sums), perm, cos, sin, both1
        )
        kvs1 = ring.gather(kv1)
        down1_own = held(down_weight[1], in1, *kvs1)
        cotangent_late = held(cotangent[0], *kvs1)
        down1 = lax.all_gather(down1_own, "wt", axis=0, tiled=True)
        middle1, normed1, heads1, mix1, lse1, turn1 = attention(
            cfg, held(query1, down1_own, cotangent_late), kvs1, own_row, kvs0, hidden1, gain1, perm, perm2, both1, QKV_W
        )
        grads1 = ring.gather(cotangent_late, normed1)
        xs1 = ring.gather(normed1)

        def feed_reduce(keep, send, x_all, ugrad, act, g_all, *sc_behind):
            total = ring.first(keep, send)
            out = ring.outgoing(total)
            got = ring.move(total, out)
            in_terms = dot_rows(held(x_all, out), ugrad).astype(bf16)
            in_part = lax.psum_scatter(
                held(in_terms, *sc_behind), "wt", scatter_dimension=0, tiled=True
            )
            total = ring.add(total, held(got, in_terms))
            while total.shape[0] > 2:
                total = ring.step(total)
            out = ring.outgoing(total)
            got = ring.move(total, out)[0]
            down_terms = dot_rows(held(act, out), g_all)[:units].astype(bf16)
            return (total[0], held(got, down_terms)), in_part, down_terms

        keep, send, g_all1, ugrad1, x_all1, act1 = feed_forward_back(xs1, None, grads1, in1, down1)
        sums, in_part1, down_terms1 = feed_reduce(keep, send, x_all1, ugrad1, act1, g_all1)
        down_part1 = lax.psum_scatter(down_terms1, "wt", scatter_dimension=0, tiled=True)
        mgrad1, low1, mlp_gain_grad1, heads_grad1 = middle_back(
            cfg, sums, middle1, cotangent[0], gain1, perm, perm2, both1, QKV_W
        )
        keep, send, part1 = attention_back(
            cfg, heads_grad1, mix1, lse1, turn1, query1, kvs1, own_row, kvs0, cos, sin
        )
        kv_total = ring.first(keep, send)
        kv_out = ring.outgoing(kv_total)
        kv_got = ring.move(kv_total, kv_out)
        query_rel1 = query_back(cfg, held(part1, kv_out), both1)
        kv_sums = ring.finish(ring.add(kv_total, held(kv_got, query_rel1)))
        kv_sums = (kv_sums[0], held(kv_sums[1], in_part1))
        grad1, grad1_low, kv_part1, attn_gain_grad1 = layer_back(
            cfg, kv_sums, query_rel1, hidden1, mgrad1, gain1, cos, sin, perm, both1
        )
        grads0 = ring.gather(grad1_low, down_part1, places=(3,))

        def wide_row(row):
            return jnp.pad(row[:1], ((0, 0), (0, QKV_W - D)))

        out_keep1, out_send1 = row_terms(heads1, held(low1, grad1_low))
        joint_keep1, joint_send1 = row_terms(
            rel1,
            jnp.concatenate([part1, kv_part1], axis=1),
            wide_row(attn_gain_grad1),
            wide_row(mlp_gain_grad1),
        )
        total1 = jnp.concatenate(
            [ring.first(out_keep1, out_send1), ring.first(joint_keep1, joint_send1)], axis=2
        )
        out1 = ring.outgoing(total1)
        cut = n // 2 * tokens
        act_late = held(act1, joint_send1)[:, :units]
        last_keep = dot(act_late[:cut], down1).astype(bf16)
        last_send = dot(act_late[cut:], down1).astype(bf16)
        hidden_total = ring.first(last_keep, last_send)
        hidden_out1 = ring.outgoing(hidden_total)
        grads0[-1] = held(grads0[-1], out1, hidden_out1)
        keep, send, g_all0, ugrad0 = feed_forward_back(None, units0, grads0, in0, down0)
        got1 = ring.move(total1, out1)
        hidden_got = ring.move(hidden_total, hidden_out1)
        sums, in_part0, down_terms0 = feed_reduce(
            keep, held(send, got1, hidden_got), x_all0, ugrad0, act0, g_all0, down_part1
        )
        mgrad0, low0, mlp_gain_grad0, heads_grad0 = middle_back(
            cfg, sums, middle0, grad1, gain0, perm, perm2, both0, QKV_W
        )
        total1 = ring.add(total1, held(got1, heads_grad0))
        while total1.shape[0] > 2:
            total1 = ring.step(total1)
        out1 = ring.outgoing(total1)
        hidden_total = ring.add(hidden_total, held(hidden_got, heads_grad0))
        while hidden_total.shape[0] > 2:
            hidden_total = ring.step(hidden_total)
        hidden_out1 = ring.outgoing(hidden_total)
        keep, send, part0 = attention_back(
            cfg, held(heads_grad0, out1, hidden_out1), mix0, lse0, turn0, query0, kvs0,
            own_row, kvs0, cos, sin,
        )
        got1 = ring.move(total1, out1)[0]
        hidden_got = ring.move(hidden_total, hidden_out1)[0]
        send = held(send, got1, hidden_got)
        kv_total = ring.first(keep, send)
        kv_out = ring.outgoing(kv_total)
        kv_got = ring.move(kv_total, kv_out)
        query_rel0 = query_back(cfg, held(part0, kv_out), both0)
        out_keep0, out_send0 = row_terms(heads0, held(low0, kv_out), mlp_gain_grad0[:1])
        kv_total = ring.add(kv_total, held(kv_got, query_rel0, out_send0))
        while kv_total.shape[0] > 2:
            kv_total = ring.step(kv_total)
        kv_out = ring.outgoing(kv_total)
        kv_got = ring.move(kv_total, kv_out)[0]
        query_keep0, query_send0 = row_terms(rel0, held(part0, kv_out))
        kv_sums = (kv_total[0], held(kv_got, query_send0))
        down_part0 = lax.psum_scatter(down_terms0, "wt", scatter_dimension=0, tiled=True)
        z_out1 = (total1[0] + held(got1, kv_got).astype(f32)).astype(bf16)
        z_out1 = z_out1.reshape(m, pad_rows, z_out1.shape[-1])
        z_got1 = [ring.swap_z(z_out1[k], k) for k in range(1, m)]
        grad0, unused, kv_part0, attn_gain_grad0 = layer_back(
            cfg, (kv_sums[0], held(kv_sums[1], in_part0, z_out1)), query_rel0, hidden0, mgrad0, gain0, cos, sin, perm, both0
        )
        hidden_out = middle1 + hidden_total[0] + held(hidden_got, grad0).astype(f32)
        first0 = jnp.concatenate(
            [
                ring.first(held(out_keep0, grad0), out_send0),
                ring.first(held(query_keep0, grad0), query_send0),
            ],
            axis=2,
        )
        first0 = ring.step(first0)
        gain_rows = jnp.pad(attn_gain_grad0[:1], ((0, 127), (0, 0))).astype(bf16)
        columns = lax.dot_general(
            perm, gain_rows, (((0,), (1,)), ((), ())), preferred_element_type=f32
        ).astype(bf16)
        cut = all_rows // 2
        kv_keep0, kv_send0 = [
            jnp.concatenate([half, columns[i * cut : (i + 1) * cut]], axis=1)
            for i, half in enumerate(row_terms(rel0, kv_part0))
        ]
        last0 = ring.first(kv_keep0, kv_send0)
        last_out0 = ring.outgoing(last0)
        last_got0 = ring.move(last0, last_out0)
        home = feed_in_home([held(in_part0, last_got0), in_part1])
        last0 = ring.add(last0, last_got0)
        total0 = jnp.concatenate([first0, last0], axis=2)
        while total0.shape[0] > 2:
            total0 = ring.step(total0)
        last_got0 = ring.move(total0, held(ring.outgoing(total0), down_part0))[0]
        last_sum0 = (total0[0] + last_got0.astype(f32)).astype(bf16)
        layer0 = ring.reduce_z(last_sum0.reshape(m, pad_rows, last_sum0.shape[-1]))
        layer1 = sum((held(g, layer0).astype(f32) for g in z_got1), z_out1[0].astype(f32))
        gain_at = QW + QKV_W

        def own_part(row, width):
            return lax.dynamic_slice(row, (0, shard * width), (1, width))[0]

        stacked = [
            jnp.stack([layer0[:rows, gain_at], own_part(layer1[rows + 1 : rows + 2, QW:], rows)]),
            jnp.stack([layer[:rows, QW : QW + QKV_W] for layer in (layer0, layer1)]),
            jnp.stack(
                [own_part(l[rows : rows + 1, QW : QW + QKV_W], bias_w) for l in (layer0, layer1)]
            ),
            jnp.stack([layer[:rows, :QW] for layer in (layer0, layer1)]),
            jnp.stack(
                [
                    own_part(layer0[rows + 1 : rows + 2, :QW], rows),
                    own_part(layer1[rows + 2 : rows + 3, QW:], rows),
                ]
            ),
        ]
        in_weight_grad = feed_in_out(held(home, last_sum0))
        down_weight_grad = jnp.stack([down_part0, down_part1]).astype(f32)
        return (hidden_out[None], grad0[None], *stacked, in_weight_grad, down_weight_grad)

    return body


def solution(mesh):
    sizes = dict(mesh.shape)
    rows = P("wt", "ctx", None)
    vector = P(None, ("ctx", "wt"))
    matrix = P(None, ("ctx", "wt"), None)
    return jax.shard_map(
        make_body(sizes["ctx"], sizes["wt"]),
        mesh=mesh,
        in_specs=(
            rows, P("wt", "ctx"), rows, vector, matrix, vector, matrix, vector, matrix, matrix,
        ),
        out_specs=(rows, rows, vector, matrix, vector, matrix, vector, matrix, matrix),
        check_vma=False,
    )
```
